32 devices in a mesh: rows: 8 (over z, x), tm: 4 (over y, core).
Axes of the slice: x: 2, y: 2, z: 4, core: 2. Of those that a mesh axis runs over, the one named last changes fastest.
Arguments:
- jacobian: bfloat16 [8, 3072, 512], P('tm', 'rows'), may hold values from -3 to 3
- rhs: bfloat16 [8, 3072], P('tm', 'rows'), may hold values from -6 to 6
- forget: float32 [8], P('tm'), may hold values from 0.99 to 1
- restart: int32 [8], P('tm'), may hold values 0 or 1
Outputs:
- factor: float32 [8, 512, 512], P('tm', 'rows')
- state: float32 [8, 512], P('tm', 'rows')
The draws below stay inside these ranges and needn't reach their ends.
All inputs are finite; a program needn't handle non-finite values. No bound on the sum of `restart` on one device may be relied on, other than what follows from the above.
Results may differ from the reference program's by a relative error of at most 0.0003.
Values sent between devices are 32-bit elements; how exact they have to be, the bound alone decides.
A program may use at most 128 MiB of HBM per device.

```python
import math
import jax
import jax.numpy as jnp
from jax import lax

W = 512
SEGS = 8
ROWS = 3072


def mixing_matrix(key, lowest):
    scale_key, jitter_key = jax.random.split(jax.random.fold_in(key, 11))
    column_scales = jnp.exp(jax.random.uniform(scale_key, (W,), jnp.float32, math.log(lowest), 0.0))
    jitter = jnp.clip(jax.random.normal(jitter_key, (W, W), jnp.float32), -4.0, 4.0) * (0.25 / math.sqrt(W))
    return column_scales[:, None] * (jnp.eye(W, dtype=jnp.float32) + jitter)


def draw_jacobian(key, part):
    lowest = 0.15
    mixing = mixing_matrix(key, lowest)
    segment_keys = jax.random.split(jax.random.fold_in(key, 7), SEGS)

    def one_segment(segment_key):
        latent_key = jax.random.fold_in(segment_key, 0)
        latent = jnp.clip(jax.random.normal(latent_key, (ROWS, W), jnp.float32), -5.0, 5.0)
        mixed = jnp.dot(latent, mixing, precision=lax.Precision.HIGHEST)
        return mixed * jnp.float32(1.0 / math.sqrt(ROWS))
    return lax.map(one_segment, segment_keys).astype(jnp.bfloat16)


def plant(entries, rng, smallest, largest):
    longest = entries.shape.index(max(entries.shape))
    spots = []
    for shift in (0, 1):
        where = [jax.random.randint(jax.random.fold_in(rng, axis), (), 0, length) for axis, length in enumerate(entries.shape)]
        where[longest] = (where[longest] + shift) % entries.shape[longest]
        spots.append(tuple(where))
    return entries.at[spots[0]].set(smallest).at[spots[1]].set(largest)


def level_of(rng, extent, pieces, low, largest):
    def one(dim, shards_of):
        draws = jax.random.uniform(jax.random.fold_in(jax.random.fold_in(rng, 6), dim), (shards_of,), jnp.float32, low / len(pieces), largest / len(pieces))
        return jnp.repeat(jnp.exp(draws), extent[dim] // shards_of).reshape((-1,) + (1,) * (len(extent) - dim - 1))

    loudness = one(*pieces[0])
    for cut in pieces[1:]:
        loudness = loudness * one(*cut)
    return loudness


def gaussian(rng, extent, width, most, shards=(), kind=jnp.bfloat16):
    drawn = width * jax.random.normal(rng, extent, jnp.float32)
    if shards:
        drawn = drawn * level_of(rng, extent, shards, -0.22, 0.18)
    return jnp.clip(drawn, -most, most).astype(kind)


def setup_inputs(seed: int = 0) -> dict:
    streams_of = jax.random.split(jax.random.key(seed), 5)
    return {
        "jacobian": draw_jacobian(jax.random.fold_in(streams_of[4], 71), 0),
        "rhs": gaussian(streams_of[1], (SEGS, ROWS), 1.0, 6.0, ((0, 4), (1, 8))),
        "forget": jnp.clip(jnp.exp(math.log(1.0) - 0.0100503262 * jax.random.uniform(streams_of[2], (SEGS,), jnp.float32) ** level_of(streams_of[2], (SEGS,), ((0, 4),), -0.2, 0.2)), 0.99, 1.0),
        "restart": plant((jax.random.randint(streams_of[3], (SEGS,), 0, 16) < 1).astype(jnp.int32), jax.random.fold_in(streams_of[3], 1), 0, 1),
    }


def segment_terms(pair):
    block, values = pair
    information = jnp.dot(block.T.astype(jnp.float32), block.astype(jnp.float32), preferred_element_type=jnp.float32)
    gradient = jnp.dot(values.astype(jnp.float32), block.astype(jnp.float32), preferred_element_type=jnp.float32)
    return (information, gradient)

def solve_one(pair):
    matrix, vector = pair
    lower_factor = jnp.linalg.cholesky(matrix)
    middle = jax.scipy.linalg.solve_triangular(lower_factor, vector, lower=True)
    result = jax.scipy.linalg.solve_triangular(lower_factor, middle, lower=True, trans=1)
    return (lower_factor.T, result)

def reference(jacobian, rhs, forget, restart):
    decays = forget * (1.0 - 0.2 * restart.astype(jnp.float32))
    information, gradient = lax.map(segment_terms, (jacobian, rhs))

    def advance(carry, inputs):
        matrix, vector = carry
        decay_now, info_now, grad_now = inputs
        matrix = decay_now * matrix + info_now
        vector = decay_now * vector + grad_now
        return ((matrix, vector), (matrix, vector))
    start = (jnp.zeros((W, W), jnp.float32), jnp.zeros((W,), jnp.float32))
    unused, posts = lax.scan(advance, start, (decays, information, gradient))
    factor, state = lax.map(solve_one, posts)
    return (factor, state)
```

```python
import functools

import jax
import jax.numpy as jnp
from jax import lax
from jax.experimental import pallas as pl
from jax.experimental.pallas import tpu as pltpu
from jax.sharding import PartitionSpec as P

HIGHEST = lax.Precision.HIGHEST
LANES = 128
GROUP = 8


def dot(a, b, over_a, over_b):
    return lax.dot_general(
        a, b, (((over_a,), (over_b,)), ((), ())),
        precision=HIGHEST, preferred_element_type=jnp.float32,
    )


def lane_spread(tile, lane):
    return jnp.broadcast_to(tile[:, lane : lane + 1], tile.shape)


def row_spread(tile, row):
    return jnp.broadcast_to(tile[row : row + 1, :], tile.shape)


def factor_tiles(many):
    lane = lax.broadcasted_iota(jnp.int32, (GROUP, LANES), 1)
    sub = lax.broadcasted_iota(jnp.int32, (GROUP, LANES), 0)
    many = [list(tiles) for tiles in many]
    count = len(many[0])
    here = range(len(many))
    over = [jnp.ones((GROUP, LANES), jnp.float32) for _ in here]
    pivots = [[None] * count for _ in here]
    for g in range(count):
        top = [many[s][g] for s in here]
        cols = [[lane_spread(top[s], g * GROUP + k) for k in range(GROUP)] for s in here]
        inverse = [[None] * GROUP for _ in here]
        rows = [[None] * GROUP for _ in here]
        heads = [[None] * GROUP for _ in here]
        for k in range(GROUP):
            at = g * GROUP + k
            for s in here:
                head = [None] * (k + 1) + [row_spread(c, k) for c in cols[s][k + 1 :]]
                pivot = row_spread(cols[s][k], k)
                inv = 1.0 / pivot
                times = jnp.where(sub > k, cols[s][k] * inv, 0.0)
                row = row_spread(top[s], k)
                row = jnp.where(lane == at, row + row, row)
                top[s] = top[s] - times * row
                for later in range(k + 1, GROUP):
                    cols[s][later] = cols[s][later] - times * head[later]
                inverse[s][k], rows[s][k], heads[s][k] = inv, row, head
                over[s] = jnp.where(lane == at, inv, over[s])
                pivots[s][g] = pivot if k == 0 else jnp.where(sub >= k, pivot, pivots[s][g])
        for s in here:
            many[s][g] = top[s]
        for v in range(g + 1, count):
            for s in here:
                tile = many[s][v]
                mine = [lane_spread(tile, g * GROUP + k) for k in range(GROUP)]
                for k in range(GROUP):
                    times = mine[k] * inverse[s][k]
                    tile = tile - times * rows[s][k]
                    for later in range(k + 1, GROUP):
                        mine[later] = mine[later] - times * heads[s][k][later]
                many[s][v] = tile
    upper, lower = [], []
    for s in here:
        ups, lows = [], []
        for g in range(count):
            scale = lax.rsqrt(pivots[s][g])
            tile = many[s][g] * scale
            at = sub + g * GROUP
            ups.append(jnp.where(lane >= at, tile, 0.0))
            lows.append(jnp.where(lane <= at, tile * over[s], 0.0))
        upper.append(ups)
        lower.append(lows)
    return upper, lower


def smoother_kernel(start_ref, mats_ref, vecs_ref, rows_ref, state_ref, work, inv, vec):
    segs, width = mats_ref.shape[0], mats_ref.shape[1]
    blocks = width // LANES
    tiles = LANES // GROUP
    for s in range(segs):
        work[s] = mats_ref[s]
        vec[s] = jnp.broadcast_to(vecs_ref[s], (GROUP, width))

    def block_step(b, carry):
        base = pl.multiple_of(b * LANES, LANES)
        square = [
            [work[s, pl.ds(pl.multiple_of(base + t * GROUP, GROUP), GROUP), pl.ds(base, LANES)] for t in range(tiles)]
            for s in range(segs)
        ]
        upper, lower = factor_tiles(square)
        for s in range(segs):
            for t in range(tiles):
                work[s, pl.ds(pl.multiple_of(base + t * GROUP, GROUP), GROUP), pl.ds(base, LANES)] = upper[s][t]
                inv[s, pl.ds(pl.multiple_of(base + t * GROUP, GROUP), GROUP), :] = lower[s][t]

        for i in range(blocks):
            @pl.when(b == i)
            def _(i=i):
                lo, hi = i * LANES, (i + 1) * LANES
                for s in range(segs):
                    low = inv[s, lo:hi, :]
                    y = dot(vec[s, :, lo:hi], low, 1, 1)
                    vec[s, :, lo:hi] = y
                    if i < blocks - 1:
                        panel = dot(low, work[s, lo:hi, hi:], 1, 0)
                        work[s, lo:hi, hi:] = panel
                        vec[s, :, hi:] = vec[s, :, hi:] - dot(y, panel, 1, 0)
                        for j in range(i + 1, blocks):
                            left = (j - i - 1) * LANES
                            jl, jh = j * LANES, (j + 1) * LANES
                            work[s, jl:jh, jl:] = work[s, jl:jh, jl:] - dot(
                                panel[:, left : left + LANES], panel[:, left:], 0, 0
                            )
                            work[s, jl:jh, lo:hi] = jnp.zeros((LANES, LANES), jnp.float32)
        return carry

    lax.fori_loop(0, blocks, block_step, 0)
    for b in reversed(range(blocks)):
        lo, hi = b * LANES, (b + 1) * LANES
        for s in range(segs):
            right = vec[s, :, lo:hi]
            if b < blocks - 1:
                right = right - dot(vec[s, :, hi:], work[s, lo:hi, hi:], 1, 1)
            vec[s, :, lo:hi] = dot(right, inv[s, lo:hi, :], 1, 0)
    share = rows_ref.shape[1]
    start = pl.multiple_of(start_ref[0], GROUP)
    for s in range(segs):
        rows_ref[s] = work[s, pl.ds(start, share), :]
        state_ref[s] = vec[s]


def smooth(mats, vecs, row_start, row_share):
    segs, width = mats.shape[0], mats.shape[1]
    vmem = pl.BlockSpec(memory_space=pltpu.VMEM)
    rows, state = pl.pallas_call(
        smoother_kernel,
        out_shape=(
            jax.ShapeDtypeStruct((segs, row_share, width), jnp.float32),
            jax.ShapeDtypeStruct((segs, GROUP, width), jnp.float32),
        ),
        in_specs=[pl.BlockSpec(memory_space=pltpu.SMEM), vmem, vmem],
        out_specs=(vmem, vmem),
        scratch_shapes=[
            pltpu.VMEM((segs, width, width), jnp.float32),
            pltpu.VMEM((segs, width, LANES), jnp.float32),
            pltpu.VMEM((segs, GROUP, width), jnp.float32),
        ],
        compiler_params=pltpu.CompilerParams(vmem_limit_bytes=40 * 1024 * 1024),
        cost_estimate=pl.CostEstimate(
            flops=2 * segs * width**3, bytes_accessed=8 * segs * width**2, transcendentals=0
        ),
    )(jnp.reshape(row_start, (1,)), mats, vecs.reshape(segs, 1, width))
    return rows, lax.dynamic_slice_in_dim(state[:, 0, :], row_start, row_share, 1)


def on_device(jacobian, rhs, forget, restart):
    segments_here, _, state_width = jacobian.shape
    row_share = state_width // lax.axis_size("rows")
    row_start = lax.axis_index("rows") * row_share
    decays = forget * (1.0 - 0.2 * restart.astype(jnp.float32))
    partial_value = jnp.einsum(
        "srv,srw->svw", jacobian, jacobian, preferred_element_type=jnp.float32
    )
    gradient = jnp.einsum("sr,srv->sv", rhs, jacobian, preferred_element_type=jnp.float32)
    both = jnp.concatenate([partial_value, gradient[:, None, :]], axis=1)
    both = lax.psum(both, "rows")
    local, retained = [both[0]], [decays[0]]
    for s in range(1, segments_here):
        local.append(decays[s] * local[-1] + both[s])
        retained.append(decays[s] * retained[-1])
    count, mine = lax.axis_size("tm"), lax.axis_index("tm")
    ends = lax.all_gather(local[-1], "tm")
    keeps = lax.all_gather(retained[-1], "tm")
    before = jnp.zeros_like(local[0])
    for t in range(count - 1):
        before = jnp.where(t < mine, keeps[t] * before + ends[t], before)
    post = jnp.stack([retained[s] * before + local[s] for s in range(segments_here)])
    return smooth(post[:, :state_width], post[:, state_width], row_start, row_share)


def solution(mesh):
    in_specs = (P("tm", "rows", None), P("tm", "rows"), P("tm"), P("tm"))
    out_specs = (P("tm", "rows", None), P("tm", "rows"))
    return jax.shard_map(
        on_device, mesh=mesh, in_specs=in_specs, out_specs=out_specs, check_vma=False
    )
```

```python
import functools

import jax
import jax.numpy as jnp
from jax import lax
from jax.experimental import pallas as pl
from jax.experimental.pallas import tpu as pltpu
from jax.sharding import PartitionSpec as P

HIGHEST = lax.Precision.HIGHEST
LANES = 128
GROUP = 8


def dot(a, b, over_a, over_b):
    return lax.dot_general(
        a, b, (((over_a,), (over_b,)), ((), ())),
        precision=HIGHEST, preferred_element_type=jnp.float32,
    )


def lane_spread(tile, lane):
    return jnp.broadcast_to(tile[:, lane : lane + 1], tile.shape)


def row_spread(tile, row):
    return jnp.broadcast_to(tile[row : row + 1, :], tile.shape)


def factor_tiles(many):
    lane = lax.broadcasted_iota(jnp.int32, (GROUP, LANES), 1)
    sub = lax.broadcasted_iota(jnp.int32, (GROUP, LANES), 0)
    many = [list(tiles) for tiles in many]
    count = len(many[0])
    here = range(len(many))
    over = [jnp.ones((GROUP, LANES), jnp.float32) for _ in here]
    pivots = [[None] * count for _ in here]
    for g in range(count):
        top = [many[s][g] for s in here]
        cols = [[lane_spread(top[s], g * GROUP + k) for k in range(GROUP)] for s in here]
        inverse = [[None] * GROUP for _ in here]
        rows = [[None] * GROUP for _ in here]
        heads = [[None] * GROUP for _ in here]
        for k in range(GROUP):
            at = g * GROUP + k
            for s in here:
                head = [None] * (k + 1) + [row_spread(c, k) for c in cols[s][k + 1 :]]
                pivot = row_spread(cols[s][k], k)
                inv = 1.0 / pivot
                times = jnp.where(sub > k, cols[s][k] * inv, 0.0)
                row = row_spread(top[s], k)
                row = jnp.where(lane == at, row + row, row)
                top[s] = top[s] - times * row
                for later in range(k + 1, GROUP):
                    cols[s][later] = cols[s][later] - times * head[later]
                inverse[s][k], rows[s][k], heads[s][k] = inv, row, head
                over[s] = jnp.where(lane == at, inv, over[s])
                pivots[s][g] = pivot if k == 0 else jnp.where(sub >= k, pivot, pivots[s][g])
        for s in here:
            many[s][g] = top[s]
        for v in range(g + 1, count):
            for s in here:
                tile = many[s][v]
                mine = [lane_spread(tile, g * GROUP + k) for k in range(GROUP)]
                for k in range(GROUP):
                    times = mine[k] * inverse[s][k]
                    tile = tile - times * rows[s][k]
                    for later in range(k + 1, GROUP):
                        mine[later] = mine[later] - times * heads[s][k][later]
                many[s][v] = tile
    upper, lower = [], []
    for s in here:
        ups, lows = [], []
        for g in range(count):
            scale = lax.rsqrt(pivots[s][g])
            tile = many[s][g] * scale
            at = sub + g * GROUP
            ups.append(jnp.where(lane >= at, tile, 0.0))
            lows.append(jnp.where(lane <= at, tile * over[s], 0.0))
        upper.append(ups)
        lower.append(lows)
    return upper, lower


def tile_list(width):
    blocks = width // LANES
    return [(i, j) for i in range(blocks) for j in range(i, blocks)]


def shard_rows(width, count):
    rows = len(tile_list(width)) * LANES + GROUP
    return -(-rows // (count * GROUP)) * GROUP


def gram_kernel(decay_ref, jac_ref, rhs_ref, out_ref):
    count, _, share, _ = out_ref.shape
    width = jac_ref.shape[2]
    tiles = tile_list(width)

    def put(seg, row, value):
        done = 0
        while done < value.shape[0]:
            owner, at = divmod(row + done, share)
            step = min(share - at, value.shape[0] - done)
            out_ref[owner, seg, at : at + step, :] = value[done : done + step, :]
            done += step

    keep = decay_ref[1]
    for i in range(width // LANES):
        lo, hi = i * LANES, (i + 1) * LANES
        first, second = [
            lax.dot_general(
                jac_ref[s, :, lo:hi], jac_ref[s, :, lo:], (((0,), (0,)), ((), ())),
                preferred_element_type=jnp.float32,
            )
            for s in range(2)
        ]
        second = keep * first + second
        for j in range(i, width // LANES):
            row = tiles.index((i, j)) * LANES
            left = (j - i) * LANES
            put(0, row, first[:, left : left + LANES])
            put(1, row, second[:, left : left + LANES])
    row = len(tiles) * LANES
    vecs = [
        jnp.dot(rhs_ref[s : s + 1, :], jac_ref[s], preferred_element_type=jnp.float32) for s in range(2)
    ]
    vecs[1] = keep * vecs[0] + vecs[1]
    for s in range(2):
        parts = [vecs[s][:, lo : lo + LANES] for lo in range(0, width, LANES)]
        pad = jnp.zeros((count * share - row - len(parts), LANES), jnp.float32)
        put(s, row, jnp.concatenate(parts + [pad], axis=0))


def gram(decays, jacobian, rhs, count):
    width = jacobian.shape[2]
    vmem = pl.BlockSpec(memory_space=pltpu.VMEM)
    return pl.pallas_call(
        gram_kernel,
        out_shape=jax.ShapeDtypeStruct((count, 2, shard_rows(width, count), LANES), jnp.float32),
        in_specs=[pl.BlockSpec(memory_space=pltpu.SMEM), vmem, vmem],
        out_specs=vmem,
        compiler_params=pltpu.CompilerParams(vmem_limit_bytes=40 * 1024 * 1024),
    )(decays, jacobian, rhs)


def exchange_kernel(
    count, steps, decay_ref, part_ref, out_ref, near, far, mine, past, post, prior, weight,
    near_send, near_recv, far_send, far_recv, past_send, past_recv, post_send, post_recv,
):
    me, now = lax.axis_index("rows"), lax.axis_index("tm")
    half, share = count // 2, out_ref.shape[1]
    line, side = me // 2, me % 2

    barrier = pltpu.get_barrier_semaphore()
    for j in range(1, count):
        pl.semaphore_signal(
            barrier, inc=1, device_id=((me + j) % count, now), device_id_type=pl.DeviceIdType.MESH
        )
    for j in range(1, steps):
        pl.semaphore_signal(
            barrier, inc=1, device_id=(me, (now + j) % steps), device_id_type=pl.DeviceIdType.MESH
        )
    pl.semaphore_wait(barrier, count + steps - 2)

    def send(src, dst, send_sem, recv_sem, row, step):
        return pltpu.make_async_remote_copy(
            src_ref=src, dst_ref=dst, send_sem=send_sem, recv_sem=recv_sem,
            device_id=(row, step), device_id_type=pl.DeviceIdType.MESH,
        )

    order = list(range(1, half)) + [0]
    first = {}
    for j in order:
        owner = 2 * ((line + j) % half) + (1 - side)
        first[j] = send(
            part_ref.at[owner], near.at[j], near_send.at[j], near_recv.at[j], 2 * line + (1 - side), now
        )
        first[j].start()
    second = {}
    for j in order:
        first[j].wait_recv()
        owner = 2 * ((line + j) % half) + side
        near[j] = near[j] + part_ref[owner]
        if j:
            second[j] = send(near.at[j], far.at[j], far_send.at[j], far_recv.at[j], owner, now)
            second[j].start()
    total = near[0]
    for j in range(1, half):
        second[j].wait_recv()
        total = total + far[j]
    keep0, keep1 = decay_ref[0], decay_ref[1]
    mine[:, :share, :] = total
    mine[:, share:, :] = jnp.full((2, GROUP, LANES), keep0 * keep1, jnp.float32)

    passed = {}
    for j in range(1, steps):
        passed[j] = send(
            mine.at[1], past.at[j], past_send.at[j], past_recv.at[j], me, (now + j) % steps
        )

        @pl.when(now + j < steps)
        def _(j=j):
            passed[j].start()

    prior[...] = jnp.zeros_like(prior)
    weight[...] = jnp.ones_like(weight)
    for j in range(1, steps):
        @pl.when(now >= j)
        def _(j=j):
            passed[j].wait_recv()
            prior[...] = prior[...] + weight[0:1, :] * past[j, :share, :]
            weight[...] = weight[...] * past[j, share:, :]

    post[0] = keep0 * prior[...] + mine[0, :share, :]
    post[1] = (keep0 * keep1) * prior[...] + mine[1, :share, :]

    last = {}
    for j in range(1, count):
        other = (me + j) % count
        last[j] = send(
            post.at[other % 2], out_ref.at[me], post_send.at[j], post_recv.at[j], other, now
        )
        last[j].start()
    out_ref[me] = post[side]
    for j in range(1, count):
        last[j].wait_recv()
    for j in order:
        first[j].wait_send()
        if j:
            second[j].wait_send()
    for j in range(1, steps):
        @pl.when(now + j < steps)
        def _(j=j):
            passed[j].wait_send()
    for j in range(1, count):
        last[j].wait_send()


def exchange(decays, parts, count, steps):
    share = parts.shape[2]
    half = count // 2
    vmem = pl.BlockSpec(memory_space=pltpu.VMEM)
    dma = pltpu.SemaphoreType.DMA
    f32 = jnp.float32
    return pl.pallas_call(
        functools.partial(exchange_kernel, count, steps),
        out_shape=jax.ShapeDtypeStruct((count, share, LANES), f32),
        in_specs=[pl.BlockSpec(memory_space=pltpu.SMEM), vmem],
        out_specs=vmem,
        scratch_shapes=[
            pltpu.VMEM((half, 2, share, LANES), f32),
            pltpu.VMEM((half, 2, share, LANES), f32),
            pltpu.VMEM((2, share + GROUP, LANES), f32),
            pltpu.VMEM((steps, share + GROUP, LANES), f32),
            pltpu.VMEM((2, share, LANES), f32),
            pltpu.VMEM((share, LANES), f32),
            pltpu.VMEM((GROUP, LANES), f32),
            dma((half,)), dma((half,)), dma((half,)), dma((half,)),
            dma((steps,)), dma((steps,)), dma((count,)), dma((count,)),
        ],
        compiler_params=pltpu.CompilerParams(
            collective_id=0, has_side_effects=True, vmem_limit_bytes=40 * 1024 * 1024
        ),
    )(decays, parts)


def smoother_kernel(place_ref, flat_ref, rows_ref, work, inv, vec):
    segs, width = work.shape[0], work.shape[1]
    blocks = width // LANES
    tiles = LANES // GROUP
    packed = tile_list(width)
    for q, (i, j) in enumerate(packed):
        work[0, i * LANES : (i + 1) * LANES, j * LANES : (j + 1) * LANES] = flat_ref[q * LANES : (q + 1) * LANES, :]
    for j in range(blocks):
        row = len(packed) * LANES + j
        vec[0, :, j * LANES : (j + 1) * LANES] = jnp.broadcast_to(flat_ref[row : row + 1, :], (GROUP, LANES))

    def block_step(b, carry):
        base = pl.multiple_of(b * LANES, LANES)
        square = [
            [work[s, pl.ds(pl.multiple_of(base + t * GROUP, GROUP), GROUP), pl.ds(base, LANES)] for t in range(tiles)]
            for s in range(segs)
        ]
        upper, lower = factor_tiles(square)
        for s in range(segs):
            for t in range(tiles):
                work[s, pl.ds(pl.multiple_of(base + t * GROUP, GROUP), GROUP), pl.ds(base, LANES)] = upper[s][t]
                inv[s, pl.ds(pl.multiple_of(base + t * GROUP, GROUP), GROUP), :] = lower[s][t]

        for i in range(blocks):
            @pl.when(b == i)
            def _(i=i):
                lo, hi = i * LANES, (i + 1) * LANES
                for s in range(segs):
                    low = inv[s, lo:hi, :]
                    y = dot(vec[s, :, lo:hi], low, 1, 1)
                    vec[s, :, lo:hi] = y
                    if i < blocks - 1:
                        panel = dot(low, work[s, lo:hi, hi:], 1, 0)
                        work[s, lo:hi, hi:] = panel
                        vec[s, :, hi:] = vec[s, :, hi:] - dot(y, panel, 1, 0)
                        for j in range(i + 1, blocks):
                            left = (j - i - 1) * LANES
                            jl, jh = j * LANES, (j + 1) * LANES
                            work[s, jl:jh, jl:] = work[s, jl:jh, jl:] - dot(
                                panel[:, left : left + LANES], panel[:, left:], 0, 0
                            )
                            work[s, jl:jh, lo:hi] = jnp.zeros((LANES, LANES), jnp.float32)
        return carry

    lax.fori_loop(0, blocks, block_step, 0)
    for b in reversed(range(blocks)):
        lo, hi = b * LANES, (b + 1) * LANES
        for s in range(segs):
            right = vec[s, :, lo:hi]
            if b < blocks - 1:
                right = right - dot(vec[s, :, hi:], work[s, lo:hi, hi:], 1, 1)
            vec[s, :, lo:hi] = dot(right, inv[s, lo:hi, :], 1, 0)
    share = rows_ref.shape[1] - GROUP
    for k in range(2):
        start = pl.multiple_of(place_ref[k], GROUP)
        rows_ref[k, :share, :] = work[0, pl.ds(start, share), :]
        rows_ref[k, share:, :] = vec[0]


def smooth(flat, width, row_start, other_start, row_share):
    vmem = pl.BlockSpec(memory_space=pltpu.VMEM)
    return pl.pallas_call(
        smoother_kernel,
        out_shape=jax.ShapeDtypeStruct((2, row_share + GROUP, width), jnp.float32),
        in_specs=[pl.BlockSpec(memory_space=pltpu.SMEM), vmem],
        out_specs=vmem,
        scratch_shapes=[
            pltpu.VMEM((1, width, width), jnp.float32),
            pltpu.VMEM((1, width, LANES), jnp.float32),
            pltpu.VMEM((1, GROUP, width), jnp.float32),
        ],
        compiler_params=pltpu.CompilerParams(vmem_limit_bytes=40 * 1024 * 1024),
        cost_estimate=pl.CostEstimate(
            flops=2 * width**3, bytes_accessed=8 * width**2, transcendentals=0
        ),
    )(jnp.stack([row_start, other_start]), flat)


def on_device(jacobian, rhs, forget, restart):
    width = jacobian.shape[2]
    count, steps = lax.axis_size("rows"), lax.axis_size("tm")
    row_share = width // count
    me = lax.axis_index("rows")
    side = me % 2
    other = me + 1 - 2 * side
    decays = forget * (1.0 - 0.2 * restart.astype(jnp.float32))
    parts = gram(decays, jacobian, rhs, count)
    flat = exchange(decays, parts, count, steps).reshape(-1, LANES)
    both = smooth(flat, width, me * row_share, other * row_share, row_share)
    swap = [(k, k + 1 - 2 * (k % 2)) for k in range(count)]
    here, there = both[0], lax.ppermute(both[1], "rows", swap)
    pair = jnp.where(side == 0, jnp.stack([here, there]), jnp.stack([there, here]))
    state = lax.dynamic_slice_in_dim(pair[:, row_share, :], me * row_share, row_share, 1)
    return pair[:, :row_share, :], state


def solution(mesh):
    in_specs = (P("tm", "rows", None), P("tm", "rows"), P("tm"), P("tm"))
    out_specs = (P("tm", "rows", None), P("tm", "rows"))
    return jax.shard_map(
        on_device, mesh=mesh, in_specs=in_specs, out_specs=out_specs, check_vma=False
    )
```

```python
import functools

import jax
import jax.numpy as jnp
from jax import lax
from jax.experimental import pallas as pl
from jax.experimental.pallas import tpu as pltpu
from jax.sharding import PartitionSpec as P

HIGHEST = lax.Precision.HIGHEST
LANES = 128
GROUP = 8


def dot(a, b, over_a, over_b):
    return lax.dot_general(
        a, b, (((over_a,), (over_b,)), ((), ())),
        precision=HIGHEST, preferred_element_type=jnp.float32,
    )


def lane_spread(tile, lane):
    return jnp.broadcast_to(tile[:, lane : lane + 1], tile.shape)


def row_spread(tile, row):
    return jnp.broadcast_to(tile[row : row + 1, :], tile.shape)


def factor_tiles(many):
    lane = lax.broadcasted_iota(jnp.int32, (GROUP, LANES), 1)
    sub = lax.broadcasted_iota(jnp.int32, (GROUP, LANES), 0)
    many = [list(tiles) for tiles in many]
    count = len(many[0])
    here = range(len(many))
    over = [jnp.ones((GROUP, LANES), jnp.float32) for _ in here]
    pivots = [[None] * count for _ in here]
    for g in range(count):
        top = [many[s][g] for s in here]
        cols = [[lane_spread(top[s], g * GROUP + k) for k in range(GROUP)] for s in here]
        inverse = [[None] * GROUP for _ in here]
        rows = [[None] * GROUP for _ in here]
        heads = [[None] * GROUP for _ in here]
        for k in range(GROUP):
            at = g * GROUP + k
            for s in here:
                head = [None] * (k + 1) + [row_spread(c, k) for c in cols[s][k + 1 :]]
                pivot = row_spread(cols[s][k], k)
                inv = 1.0 / pivot
                times = jnp.where(sub > k, cols[s][k] * inv, 0.0)
                row = row_spread(top[s], k)
                row = jnp.where(lane == at, row + row, row)
                top[s] = top[s] - times * row
                for later in range(k + 1, GROUP):
                    cols[s][later] = cols[s][later] - times * head[later]
                inverse[s][k], rows[s][k], heads[s][k] = inv, row, head
                over[s] = jnp.where(lane == at, inv, over[s])
                pivots[s][g] = pivot if k == 0 else jnp.where(sub >= k, pivot, pivots[s][g])
        for s in here:
            many[s][g] = top[s]
        for v in range(g + 1, count):
            for s in here:
                tile = many[s][v]
                mine = [lane_spread(tile, g * GROUP + k) for k in range(GROUP)]
                for k in range(GROUP):
                    times = mine[k] * inverse[s][k]
                    tile = tile - times * rows[s][k]
                    for later in range(k + 1, GROUP):
                        mine[later] = mine[later] - times * heads[s][k][later]
                many[s][v] = tile
    upper, lower = [], []
    for s in here:
        ups, lows = [], []
        for g in range(count):
            scale = lax.rsqrt(pivots[s][g])
            tile = many[s][g] * scale
            at = sub + g * GROUP
            ups.append(jnp.where(lane >= at, tile, 0.0))
            lows.append(jnp.where(lane <= at, tile * over[s], 0.0))
        upper.append(ups)
        lower.append(lows)
    return upper, lower


EARLY = ((0, 1, True), (0, 1, False), (0, 2, False), (0, 3, False))
LATE = ((1, 2, False), (1, 3, False), (2, 3, False), (2, 3, True))


def shard_rows(count):
    part = len(EARLY) * LANES // count
    return part, part + GROUP, 2 * part + GROUP


def gram_kernel(decay_ref, jac_ref, rhs_ref, out_ref):
    count = out_ref.shape[0]
    part, early, _ = shard_rows(count)
    width = jac_ref.shape[2]
    blocks = width // LANES
    keep = decay_ref[1]
    lane = lax.broadcasted_iota(jnp.int32, (LANES, LANES), 1)
    sub = lax.broadcasted_iota(jnp.int32, (LANES, LANES), 0)
    tiles = [{}, {}]
    for i in range(blocks):
        lo, hi = i * LANES, (i + 1) * LANES
        first, second = [
            lax.dot_general(
                jac_ref[s, :, lo:hi], jac_ref[s, :, lo:], (((0,), (0,)), ((), ())),
                preferred_element_type=jnp.float32,
            )
            for s in range(2)
        ]
        second = keep * first + second
        for j in range(i, blocks):
            left = (j - i) * LANES
            tiles[0][i, j] = first[:, left : left + LANES]
            tiles[1][i, j] = second[:, left : left + LANES]
    vecs = [
        jnp.dot(rhs_ref[s : s + 1, :], jac_ref[s], preferred_element_type=jnp.float32) for s in range(2)
    ]
    vecs[1] = keep * vecs[0] + vecs[1]
    for s in range(2):
        for names, base in ((EARLY, 0), (LATE, early)):
            for q, (i, j, square) in enumerate(names):
                tile = tiles[s][i, j]
                if square:
                    tile = jnp.where(lane > sub, tiles[s][i, i], tiles[s][j, j])
                for k in range(count // len(names)):
                    out_ref[q * (count // len(names)) + k, s, base : base + part, :] = tile[k * part : (k + 1) * part, :]
        extra = [vecs[s][:, lo : lo + LANES] for lo in range(0, width, LANES)]
        for i in (0, 2):
            extra.append(jnp.sum(jnp.where(lane == sub, tiles[s][i, i], 0.0), axis=0, keepdims=True))
        extra.append(jnp.zeros((GROUP - len(extra), LANES), jnp.float32))
        out_ref[0, s, part:early, :] = jnp.concatenate(extra, axis=0)
        for owner in range(1, count):
            out_ref[owner, s, part:early, :] = jnp.zeros((GROUP, LANES), jnp.float32)


def gram(decays, jacobian, rhs, count):
    vmem = pl.BlockSpec(memory_space=pltpu.VMEM)
    return pl.pallas_call(
        gram_kernel,
        out_shape=jax.ShapeDtypeStruct((count, 2, shard_rows(count)[2], LANES), jnp.float32),
        in_specs=[pl.BlockSpec(memory_space=pltpu.SMEM), vmem, vmem],
        out_specs=vmem,
        compiler_params=pltpu.CompilerParams(vmem_limit_bytes=40 * 1024 * 1024),
    )(decays, jacobian, rhs)


def smooth_kernel(
    count, steps, decay_ref, part_ref, rows_ref, state_ref,
    near, far, mine, past, post, prior, weight, front, back, work, inv, vec,
    near_send, near_recv, far_send, far_recv, past_send, past_recv,
    front_send, front_recv, back_send, back_recv, swap_send, swap_recv,
):
    me, now = lax.axis_index("rows"), lax.axis_index("tm")
    half = count // 2
    part, early, share = shard_rows(count)
    other_row = me + 1 - 2 * (me % 2)
    line, side = me // 2, me % 2

    barrier = pltpu.get_barrier_semaphore()
    for j in range(1, count):
        pl.semaphore_signal(
            barrier, inc=1, device_id=((me + j) % count, now), device_id_type=pl.DeviceIdType.MESH
        )
    for j in range(1, steps):
        pl.semaphore_signal(
            barrier, inc=1, device_id=(me, (now + j) % steps), device_id_type=pl.DeviceIdType.MESH
        )
    pl.semaphore_wait(barrier, count + steps - 2)

    def send(src, dst, send_sem, recv_sem, row, step):
        return pltpu.make_async_remote_copy(
            src_ref=src, dst_ref=dst, send_sem=send_sem, recv_sem=recv_sem,
            device_id=(row, step), device_id_type=pl.DeviceIdType.MESH,
        )

    order = list(range(1, half)) + [0]
    first = {}
    for j in order:
        owner = 2 * ((line + j) % half) + (1 - side)
        first[j] = send(
            part_ref.at[owner], near.at[j], near_send.at[j], near_recv.at[j], 2 * line + (1 - side), now
        )
        first[j].start()
    second = {}
    for j in order:
        first[j].wait_recv()
        owner = 2 * ((line + j) % half) + side
        near[j] = near[j] + part_ref[owner]
        if j:
            second[j] = send(near.at[j], far.at[j], far_send.at[j], far_recv.at[j], owner, now)
            second[j].start()
    total = near[0]
    for j in range(1, half):
        second[j].wait_recv()
        total = total + far[j]
    keep0, keep1 = decay_ref[0], decay_ref[1]
    mine[:, :share, :] = total
    mine[:, share:, :] = jnp.full((2, GROUP, LANES), keep0 * keep1, jnp.float32)

    passed = {}
    for j in range(1, steps):
        passed[j] = send(
            mine.at[1], past.at[j], past_send.at[j], past_recv.at[j], me, (now + j) % steps
        )

        @pl.when(now + j < steps)
        def _(j=j):
            passed[j].start()

    prior[...] = jnp.zeros_like(prior)
    weight[...] = jnp.ones_like(weight)
    for j in range(1, steps):
        @pl.when(now >= j)
        def _(j=j):
            passed[j].wait_recv()
            prior[...] = prior[...] + weight[0:1, :] * past[j, :share, :]
            weight[...] = weight[...] * past[j, share:, :]

    post[0] = keep0 * prior[...] + mine[0, :share, :]
    post[1] = (keep0 * keep1) * prior[...] + mine[1, :share, :]

    first_part, last_part = {}, {}
    for j in range(1, count):
        other = (me + j) % count
        first_part[j] = send(
            post.at[other % 2, pl.ds(0, early)], front.at[me], front_send.at[j], front_recv.at[j], other, now
        )
        last_part[j] = send(
            post.at[other % 2, pl.ds(early, part)], back.at[me], back_send.at[j], back_recv.at[j], other, now
        )
    for j in range(1, count):
        first_part[j].start()
    front[me] = post[side, 0:early]
    back[me] = post[side, early:]
    for j in range(1, count):
        first_part[j].wait_recv()
    for j in range(1, count):
        last_part[j].start()

    width = work.shape[1]
    blocks = width // LANES
    tiles = LANES // GROUP
    lane = lax.broadcasted_iota(jnp.int32, (LANES, LANES), 1)
    sub = lax.broadcasted_iota(jnp.int32, (LANES, LANES), 0)

    def unpack(names, source):
        every = count // len(names)
        for q, (i, j, square) in enumerate(names):
            tile = jnp.concatenate([source[q * every + k, :part, :] for k in range(every)], axis=0)
            if square:
                diagonal = front[0, part + blocks + i // 2 : part + blocks + i // 2 + 1, :]
                over = jnp.where(lane > sub, tile, 0.0)
                under = jnp.where(lane < sub, tile, 0.0)
                work[i * LANES : (i + 1) * LANES, i * LANES : (i + 1) * LANES] = (
                    over + over.T + jnp.where(lane == sub, diagonal, 0.0)
                )
                work[j * LANES : (j + 1) * LANES, j * LANES : (j + 1) * LANES] = tile - over + under.T
            else:
                work[i * LANES : (i + 1) * LANES, j * LANES : (j + 1) * LANES] = tile

    unpack(EARLY, front)
    for j in range(blocks):
        vec[:, j * LANES : (j + 1) * LANES] = jnp.broadcast_to(
            front[0, part + j : part + j + 1, :], (GROUP, LANES)
        )
    row_share = rows_ref.shape[1]
    swap = send(
        work.at[pl.ds(pl.multiple_of(other_row * row_share, GROUP), row_share)],
        rows_ref.at[side], swap_send.at[0], swap_recv.at[0], other_row, now,
    )
    swap_state = send(
        vec, state_ref.at[side], swap_send.at[1], swap_recv.at[1], other_row, now
    )

    def block_step(b, carry):
        base = pl.multiple_of(b * LANES, LANES)

        def place(t):
            return pl.ds(pl.multiple_of(base + t * GROUP, GROUP), GROUP)

        upper, lower = factor_tiles([[work[place(t), pl.ds(base, LANES)] for t in range(tiles)]])
        for t in range(tiles):
            work[place(t), pl.ds(base, LANES)] = upper[0][t]
            inv[place(t), :] = lower[0][t]

        for i in range(blocks):
            @pl.when(b == i)
            def _(i=i):
                lo, hi = i * LANES, (i + 1) * LANES
                low = inv[lo:hi, :]
                y = dot(vec[:, lo:hi], low, 1, 1)
                vec[:, lo:hi] = y
                if i < blocks - 1:
                    panel = dot(low, work[lo:hi, hi:], 1, 0)
                    work[lo:hi, hi:] = panel
                    vec[:, hi:] = vec[:, hi:] - dot(y, panel, 1, 0)
                    if i == 0:
                        for j in range(1, count):
                            last_part[j].wait_recv()
                        unpack(LATE, back)
                    for j in range(i + 1, blocks):
                        left = (j - i - 1) * LANES
                        jl, jh = j * LANES, (j + 1) * LANES
                        work[jl:jh, jl:] = work[jl:jh, jl:] - dot(
                            panel[:, left : left + LANES], panel[:, left:], 0, 0
                        )
                        work[jl:jh, lo:hi] = jnp.zeros((LANES, LANES), jnp.float32)

        @pl.when((me * row_share) // LANES == b)
        def _():
            swap.start()

        return carry

    lax.fori_loop(0, blocks, block_step, 0)
    for b in reversed(range(blocks)):
        lo, hi = b * LANES, (b + 1) * LANES
        right = vec[:, lo:hi]
        if b < blocks - 1:
            right = right - dot(vec[:, hi:], work[lo:hi, hi:], 1, 1)
        vec[:, lo:hi] = dot(right, inv[lo:hi, :], 1, 0)
    swap_state.start()
    rows_ref[side] = work[pl.ds(pl.multiple_of(me * row_share, GROUP), row_share), :]
    state_ref[side] = vec[...]

    for j in order:
        first[j].wait_send()
        if j:
            second[j].wait_send()
    for j in range(1, steps):
        @pl.when(now + j < steps)
        def _(j=j):
            passed[j].wait_send()
    for j in range(1, count):
        first_part[j].wait_send()
        last_part[j].wait_send()
    swap.wait()
    swap_state.wait()


def smooth(decays, parts, width, count, steps):
    part, early, share = shard_rows(count)
    half = count // 2
    vmem = pl.BlockSpec(memory_space=pltpu.VMEM)
    dma = pltpu.SemaphoreType.DMA
    f32 = jnp.float32
    return pl.pallas_call(
        functools.partial(smooth_kernel, count, steps),
        out_shape=(
            jax.ShapeDtypeStruct((2, width // count, width), f32),
            jax.ShapeDtypeStruct((2, GROUP, width), f32),
        ),
        in_specs=[pl.BlockSpec(memory_space=pltpu.SMEM), vmem],
        out_specs=(vmem, vmem),
        scratch_shapes=[
            pltpu.VMEM((half, 2, share, LANES), f32),
            pltpu.VMEM((half, 2, share, LANES), f32),
            pltpu.VMEM((2, share + GROUP, LANES), f32),
            pltpu.VMEM((steps, share + GROUP, LANES), f32),
            pltpu.VMEM((2, share, LANES), f32),
            pltpu.VMEM((share, LANES), f32),
            pltpu.VMEM((GROUP, LANES), f32),
            pltpu.VMEM((count, early, LANES), f32),
            pltpu.VMEM((count, part, LANES), f32),
            pltpu.VMEM((width, width), f32),
            pltpu.VMEM((width, LANES), f32),
            pltpu.VMEM((GROUP, width), f32),
            dma((half,)), dma((half,)), dma((half,)), dma((half,)),
            dma((steps,)), dma((steps,)), dma((count,)), dma((count,)),
            dma((count,)), dma((count,)), dma((2,)), dma((2,)),
        ],
        compiler_params=pltpu.CompilerParams(
            collective_id=0, has_side_effects=True, vmem_limit_bytes=40 * 1024 * 1024
        ),
    )(decays, parts)


def on_device(jacobian, rhs, forget, restart):
    width = jacobian.shape[2]
    count, steps = lax.axis_size("rows"), lax.axis_size("tm")
    row_share = width // count
    decays = forget * (1.0 - 0.2 * restart.astype(jnp.float32))
    parts = gram(decays, jacobian, rhs, count)
    factor, state = smooth(decays, parts, width, count, steps)
    start = lax.axis_index("rows") * row_share
    return factor, lax.dynamic_slice_in_dim(state[:, 0, :], start, row_share, 1)


def solution(mesh):
    in_specs = (P("tm", "rows", None), P("tm", "rows"), P("tm"), P("tm"))
    out_specs = (P("tm", "rows", None), P("tm", "rows"))
    return jax.shard_map(
        on_device, mesh=mesh, in_specs=in_specs, out_specs=out_specs, check_vma=False
    )
```

```python
import functools

import jax
import jax.numpy as jnp
from jax import lax
from jax.experimental import pallas as pl
from jax.experimental.pallas import tpu as pltpu
from jax.sharding import PartitionSpec as P

HIGHEST = lax.Precision.HIGHEST
LANES = 128
GROUP = 8


def dot(a, b, over_a, over_b):
    return lax.dot_general(
        a, b, (((over_a,), (over_b,)), ((), ())),
        precision=HIGHEST, preferred_element_type=jnp.float32,
    )


def lane_spread(tile, lane):
    return jnp.broadcast_to(tile[:, lane : lane + 1], tile.shape)


def row_spread(tile, row):
    return jnp.broadcast_to(tile[row : row + 1, :], tile.shape)


def factor_tiles(many):
    lane = lax.broadcasted_iota(jnp.int32, (GROUP, LANES), 1)
    sub = lax.broadcasted_iota(jnp.int32, (GROUP, LANES), 0)
    many = [list(tiles) for tiles in many]
    count = len(many[0])
    here = range(len(many))
    over = [jnp.ones((GROUP, LANES), jnp.float32) for _ in here]
    pivots = [[None] * count for _ in here]
    for g in range(count):
        top = [many[s][g] for s in here]
        cols = [[lane_spread(top[s], g * GROUP + k) for k in range(GROUP)] for s in here]
        inverse = [[None] * GROUP for _ in here]
        rows = [[None] * GROUP for _ in here]
        heads = [[None] * GROUP for _ in here]
        for k in range(GROUP):
            at = g * GROUP + k
            for s in here:
                head = [None] * (k + 1) + [row_spread(c, k) for c in cols[s][k + 1 :]]
                pivot = row_spread(cols[s][k], k)
                inv = 1.0 / pivot
                times = jnp.where(sub > k, cols[s][k] * inv, 0.0)
                row = row_spread(top[s], k)
                row = jnp.where(lane == at, row + row, row)
                top[s] = top[s] - times * row
                for later in range(k + 1, GROUP):
                    cols[s][later] = cols[s][later] - times * head[later]
                inverse[s][k], rows[s][k], heads[s][k] = inv, row, head
                over[s] = jnp.where(lane == at, inv, over[s])
                pivots[s][g] = pivot if k == 0 else jnp.where(sub >= k, pivot, pivots[s][g])
        for s in here:
            many[s][g] = top[s]
        for v in range(g + 1, count):
            for s in here:
                tile = many[s][v]
                mine = [lane_spread(tile, g * GROUP + k) for k in range(GROUP)]
                for k in range(GROUP):
                    times = mine[k] * inverse[s][k]
                    tile = tile - times * rows[s][k]
                    for later in range(k + 1, GROUP):
                        mine[later] = mine[later] - times * heads[s][k][later]
                many[s][v] = tile
    upper, lower = [], []
    for s in here:
        ups, lows = [], []
        for g in range(count):
            scale = lax.rsqrt(pivots[s][g])
            tile = many[s][g] * scale
            at = sub + g * GROUP
            ups.append(jnp.where(lane >= at, tile, 0.0))
            lows.append(jnp.where(lane <= at, tile * over[s], 0.0))
        upper.append(ups)
        lower.append(lows)
    return upper, lower


EARLY = ((0, 1, True), (0, 1, False), (0, 2, False), (0, 3, False))
LATE = ((1, 2, False), (1, 3, False), (2, 3, False), (2, 3, True))


def shard_rows(count):
    part = len(EARLY) * LANES // count
    return part, part + GROUP, 2 * part + GROUP


def smooth_kernel(count, steps, forget_ref, restart_ref, jac_ref, rhs_ref, rows_ref, state_ref, *scratch):
    chunks = (scratch[:16], scratch[16:32])
    weight, work, inv, vec, swap_send, swap_recv = scratch[32:]
    me, now = lax.axis_index("rows"), lax.axis_index("tm")
    half = count // 2
    part, early, share = shard_rows(count)
    line, side = me // 2, me % 2
    other_row = me + 1 - 2 * side
    keep0, keep1 = [forget_ref[k] * (1.0 - 0.2 * restart_ref[k].astype(jnp.float32)) for k in range(2)]
    lane = lax.broadcasted_iota(jnp.int32, (LANES, LANES), 1)
    sub = lax.broadcasted_iota(jnp.int32, (LANES, LANES), 0)

    barrier = pltpu.get_barrier_semaphore()
    for j in range(1, count):
        pl.semaphore_signal(
            barrier, inc=1, device_id=((me + j) % count, now), device_id_type=pl.DeviceIdType.MESH
        )
    for j in range(1, steps):
        pl.semaphore_signal(
            barrier, inc=1, device_id=(me, (now + j) % steps), device_id_type=pl.DeviceIdType.MESH
        )

    def send(src, dst, send_sem, recv_sem, row, step):
        return pltpu.make_async_remote_copy(
            src_ref=src, dst_ref=dst, send_sem=send_sem, recv_sem=recv_sem,
            device_id=(row, step), device_id_type=pl.DeviceIdType.MESH,
        )

    width = jac_ref.shape[2]
    blocks = width // LANES
    tiles = [{}, {}]

    def gram(i):
        lo, hi = i * LANES, (i + 1) * LANES
        first, second = [
            lax.dot_general(
                jac_ref[s, :, lo:hi], jac_ref[s, :, lo:], (((0,), (0,)), ((), ())),
                preferred_element_type=jnp.float32,
            )
            for s in range(2)
        ]
        second = keep1 * first + second
        for j in range(i, blocks):
            left = (j - i) * LANES
            tiles[0][i, j] = first[:, left : left + LANES]
            tiles[1][i, j] = second[:, left : left + LANES]

    def pack(names, part_ref):
        every = count // len(names)
        for s in range(2):
            for q, (i, j, square) in enumerate(names):
                tile = tiles[s][i, j]
                if square:
                    tile = jnp.where(lane > sub, tiles[s][i, i], tiles[s][j, j])
                for k in range(every):
                    part_ref[q * every + k, s, :part, :] = tile[k * part : (k + 1) * part, :]

    def pack_vectors(part_ref):
        vecs = [
            jnp.dot(rhs_ref[s : s + 1, :], jac_ref[s], preferred_element_type=jnp.float32) for s in range(2)
        ]
        vecs[1] = keep1 * vecs[0] + vecs[1]
        for s in range(2):
            extra = [vecs[s][:, lo : lo + LANES] for lo in range(0, width, LANES)]
            extra.append(jnp.sum(jnp.where(lane == sub, tiles[s][0, 0], 0.0), axis=0, keepdims=True))
            extra.append(jnp.sum(jnp.where(lane == sub, tiles[s][2, 2], 0.0), axis=0, keepdims=True))
            extra.append(jnp.zeros((GROUP - len(extra), LANES), jnp.float32))
            part_ref[0, s, part:, :] = jnp.concatenate(extra, axis=0)
            for owner in range(1, count):
                part_ref[owner, s, part:, :] = jnp.zeros((GROUP, LANES), jnp.float32)

    order = list(range(1, half)) + [0]
    first, second, passed, last = [({}, {}) for _ in range(4)]

    def pair_start(c):
        part_ref, near, near_send, near_recv = (chunks[c][0], chunks[c][1], chunks[c][8], chunks[c][9])
        for j in order:
            owner = 2 * ((line + j) % half) + (1 - side)
            first[c][j] = send(
                part_ref.at[owner], near.at[j], near_send.at[j], near_recv.at[j], other_row, now
            )
            first[c][j].start()

    def pair_finish(c, places):
        part_ref, near, far, far_send, far_recv = chunks[c][:3] + chunks[c][10:12]
        for j in places:
            first[c][j].wait_recv()
            owner = 2 * ((line + j) % half) + side
            near[j] = near[j] + part_ref[owner]
            if j:
                second[c][j] = send(near.at[j], far.at[j], far_send.at[j], far_recv.at[j], owner, now)
                second[c][j].start()

    def pass_on(c):
        near, far, mine, past, past_send, past_recv = chunks[c][1:5] + chunks[c][12:14]
        total = near[0]
        for j in range(1, half):
            second[c][j].wait_recv()
            total = total + far[j]
        size = total.shape[1]
        mine[:, :size, :] = total
        mine[:, size:, :] = jnp.full((2, GROUP, LANES), keep0 * keep1, jnp.float32)
        for j in range(1, steps):
            passed[c][j] = send(
                mine.at[1], past.at[j], past_send.at[j], past_recv.at[j], me, (now + j) % steps
            )

            @pl.when(now + j < steps)
            def _(j=j):
                passed[c][j].start()

    def spread(c):
        mine, past, post, prior, whole, last_send, last_recv = chunks[c][3:8] + chunks[c][14:16]
        size = post.shape[1]
        prior[...] = jnp.zeros_like(prior)
        weight[...] = jnp.ones_like(weight)
        for j in range(1, steps):
            @pl.when(now >= j)
            def _(j=j):
                passed[c][j].wait_recv()
                prior[...] = prior[...] + weight[0:1, :] * past[j, :size, :]
                weight[...] = weight[...] * past[j, size:, :]

        post[0] = keep0 * prior[...] + mine[0, :size, :]
        post[1] = (keep0 * keep1) * prior[...] + mine[1, :size, :]
        for j in range(1, count):
            other = (me + j) % count
            last[c][j] = send(
                post.at[other % 2], whole.at[me], last_send.at[j], last_recv.at[j], other, now
            )
            last[c][j].start()
        whole[me] = post[side]

    gram(0)
    gram(1)
    pack(EARLY, chunks[0][0])
    gram(2)
    pack_vectors(chunks[0][0])
    pl.semaphore_wait(barrier, count + steps - 2)
    pair_start(0)
    gram(3)
    pack(LATE, chunks[1][0])
    pair_start(1)
    pair_finish(0, order)
    pair_finish(1, order[: half // 2])
    pass_on(0)
    pair_finish(1, order[half // 2 :])
    spread(0)
    pass_on(1)
    spread(1)
    front, back = chunks[0][7], chunks[1][7]
    for j in range(1, count):
        last[0][j].wait_recv()

    tiles = LANES // GROUP

    def unpack(names, source):
        every = count // len(names)
        for q, (i, j, square) in enumerate(names):
            tile = jnp.concatenate([source[q * every + k, :part, :] for k in range(every)], axis=0)
            if square:
                diagonal = front[0, part + blocks + i // 2 : part + blocks + i // 2 + 1, :]
                over = jnp.where(lane > sub, tile, 0.0)
                under = jnp.where(lane < sub, tile, 0.0)
                work[i * LANES : (i + 1) * LANES, i * LANES : (i + 1) * LANES] = (
                    over + over.T + jnp.where(lane == sub, diagonal, 0.0)
                )
                work[j * LANES : (j + 1) * LANES, j * LANES : (j + 1) * LANES] = tile - over + under.T
            else:
                work[i * LANES : (i + 1) * LANES, j * LANES : (j + 1) * LANES] = tile

    unpack(EARLY, front)
    for j in range(blocks):
        vec[:, j * LANES : (j + 1) * LANES] = jnp.broadcast_to(
            front[0, part + j : part + j + 1, :], (GROUP, LANES)
        )
    row_share = rows_ref.shape[1]
    swap = send(
        work.at[pl.ds(pl.multiple_of(other_row * row_share, GROUP), row_share)],
        rows_ref.at[side], swap_send.at[0], swap_recv.at[0], other_row, now,
    )
    swap_state = send(
        vec, state_ref.at[side], swap_send.at[1], swap_recv.at[1], other_row, now
    )

    def block_step(b, carry):
        base = pl.multiple_of(b * LANES, LANES)

        def place(t):
            return pl.ds(pl.multiple_of(base + t * GROUP, GROUP), GROUP)

        upper, lower = factor_tiles([[work[place(t), pl.ds(base, LANES)] for t in range(tiles)]])
        for t in range(tiles):
            work[place(t), pl.ds(base, LANES)] = upper[0][t]
            inv[place(t), :] = lower[0][t]

        for i in range(blocks):
            @pl.when(b == i)
            def _(i=i):
                lo, hi = i * LANES, (i + 1) * LANES
                low = inv[lo:hi, :]
                y = dot(vec[:, lo:hi], low, 1, 1)
                vec[:, lo:hi] = y
                if i < blocks - 1:
                    panel = dot(low, work[lo:hi, hi:], 1, 0)
                    work[lo:hi, hi:] = panel
                    vec[:, hi:] = vec[:, hi:] - dot(y, panel, 1, 0)
                    if i == 0:
                        for j in range(1, count):
                            last[1][j].wait_recv()
                        unpack(LATE, back)
                    for j in range(i + 1, blocks):
                        left = (j - i - 1) * LANES
                        jl, jh = j * LANES, (j + 1) * LANES
                        work[jl:jh, jl:] = work[jl:jh, jl:] - dot(
                            panel[:, left : left + LANES], panel[:, left:], 0, 0
                        )
                        work[jl:jh, lo:hi] = jnp.zeros((LANES, LANES), jnp.float32)

        @pl.when((me * row_share) // LANES == b)
        def _():
            swap.start()

        return carry

    lax.fori_loop(0, blocks, block_step, 0)
    for b in reversed(range(blocks)):
        lo, hi = b * LANES, (b + 1) * LANES
        right = vec[:, lo:hi]
        if b < blocks - 1:
            right = right - dot(vec[:, hi:], work[lo:hi, hi:], 1, 1)
        vec[:, lo:hi] = dot(right, inv[lo:hi, :], 1, 0)
    swap_state.start()
    rows_ref[side] = work[pl.ds(pl.multiple_of(me * row_share, GROUP), row_share), :]
    state_ref[side] = vec[...]

    for c in range(2):
        for j in order:
            first[c][j].wait_send()
            if j:
                second[c][j].wait_send()
        for j in range(1, steps):
            @pl.when(now + j < steps)
            def _(j=j):
                passed[c][j].wait_send()
        for j in range(1, count):
            last[c][j].wait_send()
    swap.wait()
    swap_state.wait()


def smooth(forget, restart, jacobian, rhs, count, steps):
    width = jacobian.shape[2]
    part, early, _ = shard_rows(count)
    half = count // 2
    vmem = pl.BlockSpec(memory_space=pltpu.VMEM)
    smem = pl.BlockSpec(memory_space=pltpu.SMEM)
    dma = pltpu.SemaphoreType.DMA
    f32 = jnp.float32
    scratch = []
    for size in (early, part):
        scratch += [
            pltpu.VMEM((count, 2, size, LANES), f32),
            pltpu.VMEM((half, 2, size, LANES), f32),
            pltpu.VMEM((half, 2, size, LANES), f32),
            pltpu.VMEM((2, size + GROUP, LANES), f32),
            pltpu.VMEM((steps, size + GROUP, LANES), f32),
            pltpu.VMEM((2, size, LANES), f32),
            pltpu.VMEM((size, LANES), f32),
            pltpu.VMEM((count, size, LANES), f32),
            dma((half,)), dma((half,)), dma((half,)), dma((half,)),
            dma((steps,)), dma((steps,)), dma((count,)), dma((count,)),
        ]
    scratch += [
        pltpu.VMEM((GROUP, LANES), f32),
        pltpu.VMEM((width, width), f32),
        pltpu.VMEM((width, LANES), f32),
        pltpu.VMEM((GROUP, width), f32),
        dma((2,)), dma((2,)),
    ]
    return pl.pallas_call(
        functools.partial(smooth_kernel, count, steps),
        out_shape=(
            jax.ShapeDtypeStruct((2, width // count, width), f32),
            jax.ShapeDtypeStruct((2, GROUP, width), f32),
        ),
        in_specs=[smem, smem, vmem, vmem],
        out_specs=(vmem, vmem),
        scratch_shapes=scratch,
        compiler_params=pltpu.CompilerParams(
            collective_id=0, has_side_effects=True, vmem_limit_bytes=40 * 1024 * 1024
        ),
    )(forget, restart, jacobian, rhs)


def on_device(jacobian, rhs, forget, restart):
    count, steps = lax.axis_size("rows"), lax.axis_size("tm")
    row_share = jacobian.shape[2] // count
    factor, state = smooth(forget, restart, jacobian, rhs, count, steps)
    start = lax.axis_index("rows") * row_share
    return factor, lax.dynamic_slice_in_dim(state[:, 0, :], start, row_share, 1)


def solution(mesh):
    in_specs = (P("tm", "rows", None), P("tm", "rows"), P("tm"), P("tm"))
    out_specs = (P("tm", "rows", None), P("tm", "rows"))
    return jax.shard_map(
        on_device, mesh=mesh, in_specs=in_specs, out_specs=out_specs, check_vma=False
    )
```

```python
import functools

import jax
import jax.numpy as jnp
from jax import lax
from jax.experimental import pallas as pl
from jax.experimental.pallas import tpu as pltpu
from jax.sharding import PartitionSpec as P

HIGHEST = lax.Precision.HIGHEST
LANES = 128
GROUP = 8


def dot(a, b, over_a, over_b):
    return lax.dot_general(
        a, b, (((over_a,), (over_b,)), ((), ())),
        precision=HIGHEST, preferred_element_type=jnp.float32,
    )


def lane_spread(tile, lane):
    return jnp.broadcast_to(tile[:, lane : lane + 1], tile.shape)


def row_spread(tile, row):
    return jnp.broadcast_to(tile[row : row + 1, :], tile.shape)


def factor_tiles(many):
    lane = lax.broadcasted_iota(jnp.int32, (GROUP, LANES), 1)
    sub = lax.broadcasted_iota(jnp.int32, (GROUP, LANES), 0)
    many = [list(tiles) for tiles in many]
    count = len(many[0])
    here = range(len(many))
    over = [jnp.ones((GROUP, LANES), jnp.float32) for _ in here]
    pivots = [[None] * count for _ in here]
    for g in range(count):
        top = [many[s][g] for s in here]
        cols = [[lane_spread(top[s], g * GROUP + k) for k in range(GROUP)] for s in here]
        inverse = [[None] * GROUP for _ in here]
        rows = [[None] * GROUP for _ in here]
        heads = [[None] * GROUP for _ in here]
        for k in range(GROUP):
            at = g * GROUP + k
            for s in here:
                head = [None] * (k + 1) + [row_spread(c, k) for c in cols[s][k + 1 :]]
                pivot = row_spread(cols[s][k], k)
                inv = 1.0 / pivot
                times = jnp.where(sub > k, cols[s][k] * inv, 0.0)
                row = row_spread(top[s], k)
                row = jnp.where(lane == at, row + row, row)
                top[s] = top[s] - times * row
                for later in range(k + 1, GROUP):
                    cols[s][later] = cols[s][later] - times * head[later]
                inverse[s][k], rows[s][k], heads[s][k] = inv, row, head
                over[s] = jnp.where(lane == at, inv, over[s])
                pivots[s][g] = pivot if k == 0 else jnp.where(sub >= k, pivot, pivots[s][g])
        for s in here:
            many[s][g] = top[s]
        for v in range(g + 1, count):
            for s in here:
                tile = many[s][v]
                mine = [lane_spread(tile, g * GROUP + k) for k in range(GROUP)]
                for k in range(GROUP):
                    times = mine[k] * inverse[s][k]
                    tile = tile - times * rows[s][k]
                    for later in range(k + 1, GROUP):
                        mine[later] = mine[later] - times * heads[s][k][later]
                many[s][v] = tile
    upper, lower = [], []
    for s in here:
        ups, lows = [], []
        for g in range(count):
            scale = lax.rsqrt(pivots[s][g])
            tile = many[s][g] * scale
            at = sub + g * GROUP
            ups.append(jnp.where(lane >= at, tile, 0.0))
            lows.append(jnp.where(lane <= at, tile * over[s], 0.0))
        upper.append(ups)
        lower.append(lows)
    return upper, lower


EARLY = ((0, 1, True), (0, 1, False), (0, 2, False), (0, 3, False))
LATE = ((1, 2, False), (1, 3, False), (2, 3, False), (2, 3, True))


def shard_rows(count):
    part = len(EARLY) * LANES // count
    return part, part + GROUP, 2 * part + GROUP


def smooth_kernel(count, steps, forget_ref, restart_ref, jac_ref, rhs_ref, rows_ref, state_ref, *scratch):
    chunks = (scratch[:16], scratch[16:32])
    weight, work, inv, vec, rows_send, rows_recv, state_send, state_recv = scratch[32:]
    me, now = lax.axis_index("rows"), lax.axis_index("tm")
    half = count // 2
    part, early, share = shard_rows(count)
    line, side = me // 2, me % 2
    other_row = me + 1 - 2 * side

    def inner(row):
        return jnp.logical_or((row // 2) % 4 == 1, (row // 2) % 4 == 2)

    factors = inner(me)
    guest = 2 * jnp.where(line % 4 == 1, line - 1, jnp.minimum(line + 1, half - 1))
    takers = (other_row, guest, guest + 1)
    keep0, keep1 = [forget_ref[k] * (1.0 - 0.2 * restart_ref[k].astype(jnp.float32)) for k in range(2)]
    lane = lax.broadcasted_iota(jnp.int32, (LANES, LANES), 1)
    sub = lax.broadcasted_iota(jnp.int32, (LANES, LANES), 0)

    barrier = pltpu.get_barrier_semaphore()
    for j in range(1, count):
        pl.semaphore_signal(
            barrier, inc=1, device_id=((me + j) % count, now), device_id_type=pl.DeviceIdType.MESH
        )
    for j in range(1, steps):
        pl.semaphore_signal(
            barrier, inc=1, device_id=(me, (now + j) % steps), device_id_type=pl.DeviceIdType.MESH
        )

    def send(src, dst, send_sem, recv_sem, row, step):
        return pltpu.make_async_remote_copy(
            src_ref=src, dst_ref=dst, send_sem=send_sem, recv_sem=recv_sem,
            device_id=(row, step), device_id_type=pl.DeviceIdType.MESH,
        )

    width = jac_ref.shape[2]
    blocks = width // LANES
    tiles = [{}, {}]

    def gram(i):
        lo, hi = i * LANES, (i + 1) * LANES
        first, second = [
            lax.dot_general(
                jac_ref[s, :, lo:hi], jac_ref[s, :, lo:], (((0,), (0,)), ((), ())),
                preferred_element_type=jnp.float32,
            )
            for s in range(2)
        ]
        second = keep1 * first + second
        for j in range(i, blocks):
            left = (j - i) * LANES
            tiles[0][i, j] = first[:, left : left + LANES]
            tiles[1][i, j] = second[:, left : left + LANES]

    def pack(names, part_ref):
        every = count // len(names)
        for s in range(2):
            for q, (i, j, square) in enumerate(names):
                tile = tiles[s][i, j]
                if square:
                    tile = jnp.where(lane > sub, tiles[s][i, i], tiles[s][j, j])
                for k in range(every):
                    part_ref[q * every + k, s, :part, :] = tile[k * part : (k + 1) * part, :]

    def pack_vectors(part_ref):
        vecs = [
            jnp.dot(rhs_ref[s : s + 1, :], jac_ref[s], preferred_element_type=jnp.float32) for s in range(2)
        ]
        vecs[1] = keep1 * vecs[0] + vecs[1]
        for s in range(2):
            extra = [vecs[s][:, lo : lo + LANES] for lo in range(0, width, LANES)]
            extra.append(jnp.sum(jnp.where(lane == sub, tiles[s][0, 0], 0.0), axis=0, keepdims=True))
            extra.append(jnp.sum(jnp.where(lane == sub, tiles[s][2, 2], 0.0), axis=0, keepdims=True))
            extra.append(jnp.zeros((GROUP - len(extra), LANES), jnp.float32))
            part_ref[0, s, part:, :] = jnp.concatenate(extra, axis=0)
            for owner in range(1, count):
                part_ref[owner, s, part:, :] = jnp.zeros((GROUP, LANES), jnp.float32)

    order = list(range(1, half)) + [0]
    first, second, passed, last = [({}, {}) for _ in range(4)]

    def pair_start(c):
        part_ref, near, near_send, near_recv = (chunks[c][0], chunks[c][1], chunks[c][8], chunks[c][9])
        for j in order:
            owner = 2 * ((line + j) % half) + (1 - side)
            first[c][j] = send(
                part_ref.at[owner], near.at[j], near_send.at[j], near_recv.at[j], other_row, now
            )
            first[c][j].start()

    def pair_finish(c, places):
        part_ref, near, far, far_send, far_recv = chunks[c][:3] + chunks[c][10:12]
        for j in places:
            first[c][j].wait_recv()
            owner = 2 * ((line + j) % half) + side
            near[j] = near[j] + part_ref[owner]
            if j:
                second[c][j] = send(near.at[j], far.at[j], far_send.at[j], far_recv.at[j], owner, now)
                second[c][j].start()

    def pass_on(c):
        near, far, mine, past, past_send, past_recv = chunks[c][1:5] + chunks[c][12:14]
        total = near[0]
        for j in range(1, half):
            second[c][j].wait_recv()
            total = total + far[j]
        size = total.shape[1]
        mine[:, :size, :] = total
        mine[:, size:, :] = jnp.full((2, GROUP, LANES), keep0 * keep1, jnp.float32)
        for j in range(1, steps):
            passed[c][j] = send(
                mine.at[1], past.at[j], past_send.at[j], past_recv.at[j], me, (now + j) % steps
            )

            @pl.when(now + j < steps)
            def _(j=j):
                passed[c][j].start()

    def spread(c):
        mine, past, post, prior, whole, last_send, last_recv = chunks[c][3:8] + chunks[c][14:16]
        size = post.shape[1]
        prior[...] = jnp.zeros_like(prior)
        weight[...] = jnp.ones_like(weight)
        for j in range(1, steps):
            @pl.when(now >= j)
            def _(j=j):
                passed[c][j].wait_recv()
                prior[...] = prior[...] + weight[0:1, :] * past[j, :size, :]
                weight[...] = weight[...] * past[j, size:, :]

        post[0] = keep0 * prior[...] + mine[0, :size, :]
        post[1] = (keep0 * keep1) * prior[...] + mine[1, :size, :]
        for j in range(1, count):
            other = (me + j) % count
            last[c][j] = send(
                post.at[other % 2], whole.at[me], last_send.at[j], last_recv.at[j], other, now
            )

            @pl.when(inner(other))
            def _(j=j):
                last[c][j].start()

        whole[me] = post[side]

    gram(0)
    gram(1)
    pack(EARLY, chunks[0][0])
    gram(2)
    pack_vectors(chunks[0][0])
    pl.semaphore_wait(barrier, count + steps - 2)
    pair_start(0)
    gram(3)
    pack(LATE, chunks[1][0])
    pair_start(1)
    pair_finish(0, order)
    pair_finish(1, order[: half // 2])
    pass_on(0)
    pair_finish(1, order[half // 2 :])
    spread(0)
    pass_on(1)
    spread(1)
    front, back = chunks[0][7], chunks[1][7]
    tiles = LANES // GROUP

    def unpack(names, source):
        every = count // len(names)
        for q, (i, j, square) in enumerate(names):
            tile = jnp.concatenate([source[q * every + k, :part, :] for k in range(every)], axis=0)
            if square:
                diagonal = front[0, part + blocks + i // 2 : part + blocks + i // 2 + 1, :]
                over = jnp.where(lane > sub, tile, 0.0)
                under = jnp.where(lane < sub, tile, 0.0)
                work[i * LANES : (i + 1) * LANES, i * LANES : (i + 1) * LANES] = (
                    over + over.T + jnp.where(lane == sub, diagonal, 0.0)
                )
                work[j * LANES : (j + 1) * LANES, j * LANES : (j + 1) * LANES] = tile - over + under.T
            else:
                work[i * LANES : (i + 1) * LANES, j * LANES : (j + 1) * LANES] = tile

    row_share = rows_ref.shape[1]

    def rows_to(k, i):
        start = pl.multiple_of(takers[k] * row_share, GROUP)
        return send(
            work.at[pl.ds(start, row_share), pl.ds(i * LANES, width - i * LANES)],
            rows_ref.at[side, :, pl.ds(i * LANES, width - i * LANES)],
            rows_send.at[k], rows_recv.at[side], takers[k], now,
        )

    def state_to(k):
        return send(vec, state_ref.at[side], state_send.at[k], state_recv.at[side], takers[k], now)

    def give_rows(i):
        for k in range(3):
            @pl.when((takers[k] * row_share) // LANES == i)
            def _(k=k):
                rows_to(k, i).start()

    for i in range(1, blocks):
        @pl.when((me * row_share) // LANES == i)
        def _(i=i):
            rows_ref[:, :, : i * LANES] = jnp.zeros((2, row_share, i * LANES), jnp.float32)

    @pl.when(factors)
    def _():
        for j in range(1, count):
            last[0][j].wait_recv()
        unpack(EARLY, front)
        for j in range(blocks):
            vec[:, j * LANES : (j + 1) * LANES] = jnp.broadcast_to(
                front[0, part + j : part + j + 1, :], (GROUP, LANES)
            )

        def block_step(b, carry):
            base = pl.multiple_of(b * LANES, LANES)

            def place(t):
                return pl.ds(pl.multiple_of(base + t * GROUP, GROUP), GROUP)

            upper, lower = factor_tiles([[work[place(t), pl.ds(base, LANES)] for t in range(tiles)]])
            for t in range(tiles):
                work[place(t), pl.ds(base, LANES)] = upper[0][t]
                inv[place(t), :] = lower[0][t]

            for i in range(blocks):
                @pl.when(b == i)
                def _(i=i):
                    lo, hi = i * LANES, (i + 1) * LANES
                    low = inv[lo:hi, :]
                    y = dot(vec[:, lo:hi], low, 1, 1)
                    vec[:, lo:hi] = y
                    if i < blocks - 1:
                        panel = dot(low, work[lo:hi, hi:], 1, 0)
                        work[lo:hi, hi:] = panel
                        vec[:, hi:] = vec[:, hi:] - dot(y, panel, 1, 0)
                    give_rows(i)
                    if i < blocks - 1:
                        if i == 0:
                            for j in range(1, count):
                                last[1][j].wait_recv()
                            unpack(LATE, back)
                        for j in range(i + 1, blocks):
                            left = (j - i - 1) * LANES
                            jl, jh = j * LANES, (j + 1) * LANES
                            work[jl:jh, jl:] = work[jl:jh, jl:] - dot(
                                panel[:, left : left + LANES], panel[:, left:], 0, 0
                            )
                            work[jl:jh, lo:hi] = jnp.zeros((LANES, LANES), jnp.float32)

            return carry

        lax.fori_loop(0, blocks, block_step, 0)
        for b in reversed(range(blocks)):
            lo, hi = b * LANES, (b + 1) * LANES
            right = vec[:, lo:hi]
            if b < blocks - 1:
                right = right - dot(vec[:, hi:], work[lo:hi, hi:], 1, 1)
            vec[:, lo:hi] = dot(right, inv[lo:hi, :], 1, 0)
        for k in range(3):
            state_to(k).start()
        for i in range(blocks):
            @pl.when((me * row_share) // LANES == i)
            def _(i=i):
                start = pl.multiple_of(me * row_share, GROUP)
                rows_ref[side, :, i * LANES :] = work[pl.ds(start, row_share), i * LANES :]
        state_ref[side] = vec[...]
        for k in range(3):
            for i in range(blocks):
                @pl.when((takers[k] * row_share) // LANES == i)
                def _(k=k, i=i):
                    rows_to(k, i).wait_send()
            state_to(k).wait_send()

    for s in range(2):
        @pl.when(jnp.logical_or(jnp.logical_not(factors), side != s))
        def _(s=s):
            for i in range(blocks):
                @pl.when((me * row_share) // LANES == i)
                def _(i=i):
                    kept = rows_ref.at[s, :, pl.ds(i * LANES, width - i * LANES)]
                    send(kept, kept, rows_send.at[0], rows_recv.at[s], other_row, now).wait_recv()
            kept = state_ref.at[s]
            send(kept, kept, state_send.at[0], state_recv.at[s], other_row, now).wait_recv()

    for c in range(2):
        for j in order:
            first[c][j].wait_send()
            if j:
                second[c][j].wait_send()
        for j in range(1, steps):
            @pl.when(now + j < steps)
            def _(j=j):
                passed[c][j].wait_send()
        for j in range(1, count):
            @pl.when(inner((me + j) % count))
            def _(j=j):
                last[c][j].wait_send()


def smooth(forget, restart, jacobian, rhs, count, steps):
    width = jacobian.shape[2]
    part, early, _ = shard_rows(count)
    half = count // 2
    vmem = pl.BlockSpec(memory_space=pltpu.VMEM)
    smem = pl.BlockSpec(memory_space=pltpu.SMEM)
    dma = pltpu.SemaphoreType.DMA
    f32 = jnp.float32
    scratch = []
    for size in (early, part):
        scratch += [
            pltpu.VMEM((count, 2, size, LANES), f32),
            pltpu.VMEM((half, 2, size, LANES), f32),
            pltpu.VMEM((half, 2, size, LANES), f32),
            pltpu.VMEM((2, size + GROUP, LANES), f32),
            pltpu.VMEM((steps, size + GROUP, LANES), f32),
            pltpu.VMEM((2, size, LANES), f32),
            pltpu.VMEM((size, LANES), f32),
            pltpu.VMEM((count, size, LANES), f32),
            dma((half,)), dma((half,)), dma((half,)), dma((half,)),
            dma((steps,)), dma((steps,)), dma((count,)), dma((count,)),
        ]
    scratch += [
        pltpu.VMEM((GROUP, LANES), f32),
        pltpu.VMEM((width, width), f32),
        pltpu.VMEM((width, LANES), f32),
        pltpu.VMEM((GROUP, width), f32),
        dma((3,)), dma((2,)), dma((3,)), dma((2,)),
    ]
    return pl.pallas_call(
        functools.partial(smooth_kernel, count, steps),
        out_shape=(
            jax.ShapeDtypeStruct((2, width // count, width), f32),
            jax.ShapeDtypeStruct((2, GROUP, width), f32),
        ),
        in_specs=[smem, smem, vmem, vmem],
        out_specs=(vmem, vmem),
        scratch_shapes=scratch,
        compiler_params=pltpu.CompilerParams(
            collective_id=0, has_side_effects=True, vmem_limit_bytes=40 * 1024 * 1024
        ),
    )(forget, restart, jacobian, rhs)


def on_device(jacobian, rhs, forget, restart):
    count, steps = lax.axis_size("rows"), lax.axis_size("tm")
    row_share = jacobian.shape[2] // count
    factor, state = smooth(forget, restart, jacobian, rhs, count, steps)
    start = lax.axis_index("rows") * row_share
    return factor, lax.dynamic_slice_in_dim(state[:, 0, :], start, row_share, 1)


def solution(mesh):
    in_specs = (P("tm", "rows", None), P("tm", "rows"), P("tm"), P("tm"))
    out_specs = (P("tm", "rows", None), P("tm", "rows"))
    return jax.shard_map(
        on_device, mesh=mesh, in_specs=in_specs, out_specs=out_specs, check_vma=False
    )
```

```python
import functools

import jax
import jax.numpy as jnp
from jax import lax
from jax.experimental import pallas as pl
from jax.experimental.pallas import tpu as pltpu
from jax.sharding import PartitionSpec as P

HIGHEST = lax.Precision.HIGHEST
LANES = 128
GROUP = 8


def dot(a, b, over_a, over_b):
    return lax.dot_general(
        a, b, (((over_a,), (over_b,)), ((), ())),
        precision=HIGHEST, preferred_element_type=jnp.float32,
    )


def lane_spread(tile, lane):
    return jnp.broadcast_to(tile[:, lane : lane + 1], tile.shape)


def row_spread(tile, row):
    return jnp.broadcast_to(tile[row : row + 1, :], tile.shape)


def factor_tiles(many):
    lane = lax.broadcasted_iota(jnp.int32, (GROUP, LANES), 1)
    sub = lax.broadcasted_iota(jnp.int32, (GROUP, LANES), 0)
    many = [list(tiles) for tiles in many]
    count = len(many[0])
    here = range(len(many))
    over = [jnp.ones((GROUP, LANES), jnp.float32) for _ in here]
    pivots = [[None] * count for _ in here]
    for g in range(count):
        top = [many[s][g] for s in here]
        cols = [[lane_spread(top[s], g * GROUP + k) for k in range(GROUP)] for s in here]
        inverse = [[None] * GROUP for _ in here]
        rows = [[None] * GROUP for _ in here]
        heads = [[None] * GROUP for _ in here]
        square = [
            {(i, k): row_spread(cols[s][k], i) for k in range(GROUP) for i in range(k, GROUP)} for s in here
        ]
        for k in range(GROUP):
            at = g * GROUP + k
            for s in here:
                head = [None] * (k + 1) + [square[s][i, k] for i in range(k + 1, GROUP)]
                pivot = square[s][k, k]
                inv = 1.0 / pivot
                for i in range(k + 1, GROUP):
                    share = square[s][i, k] * inv
                    for j in range(k + 1, i + 1):
                        square[s][i, j] = square[s][i, j] - share * square[s][j, k]
                times = jnp.where(sub > k, cols[s][k] * inv, 0.0)
                row = row_spread(top[s], k)
                row = jnp.where(lane == at, row + row, row)
                top[s] = top[s] - times * row
                for later in range(k + 1, GROUP):
                    cols[s][later] = cols[s][later] - times * head[later]
                inverse[s][k], rows[s][k], heads[s][k] = inv, row, head
                over[s] = jnp.where(lane == at, inv, over[s])
                pivots[s][g] = pivot if k == 0 else jnp.where(sub >= k, pivot, pivots[s][g])
        for s in here:
            many[s][g] = top[s]
        for v in range(g + 1, count):
            for s in here:
                tile = many[s][v]
                mine = [lane_spread(tile, g * GROUP + k) for k in range(GROUP)]
                for k in range(GROUP):
                    times = mine[k] * inverse[s][k]
                    tile = tile - times * rows[s][k]
                    for later in range(k + 1, GROUP):
                        mine[later] = mine[later] - times * heads[s][k][later]
                many[s][v] = tile
    upper, lower = [], []
    for s in here:
        ups, lows = [], []
        for g in range(count):
            scale = lax.rsqrt(pivots[s][g])
            tile = many[s][g] * scale
            at = sub + g * GROUP
            ups.append(jnp.where(lane >= at, tile, 0.0))
            lows.append(jnp.where(lane <= at, tile * over[s], 0.0))
        upper.append(ups)
        lower.append(lows)
    return upper, lower


EARLY = ((0, 1, True), (0, 1, False), (0, 2, False), (0, 3, False))
LATE = ((1, 2, False), (1, 3, False), (2, 3, False), (2, 3, True))


def shard_rows(count):
    part = len(EARLY) * LANES // count
    return part, part + GROUP, 2 * part + GROUP


def smooth_kernel(count, steps, forget_ref, restart_ref, jac_ref, rhs_ref, rows_ref, state_ref, *scratch):
    chunks = (scratch[:16], scratch[16:32])
    weight, work, inv, vec, rows_send, rows_recv, state_send, state_recv = scratch[32:]
    me, now = lax.axis_index("rows"), lax.axis_index("tm")
    half = count // 2
    part, early, share = shard_rows(count)
    line, side = me // 2, me % 2
    other_row = me + 1 - 2 * side

    def inner(row):
        return jnp.logical_or((row // 2) % 4 == 1, (row // 2) % 4 == 2)

    factors = inner(me)
    guest = 2 * jnp.where(line % 4 == 1, line - 1, jnp.minimum(line + 1, half - 1))
    takers = (other_row, guest, guest + 1)
    keep0, keep1 = [forget_ref[k] * (1.0 - 0.2 * restart_ref[k].astype(jnp.float32)) for k in range(2)]
    lane = lax.broadcasted_iota(jnp.int32, (LANES, LANES), 1)
    sub = lax.broadcasted_iota(jnp.int32, (LANES, LANES), 0)

    barrier = pltpu.get_barrier_semaphore()
    for j in range(1, count):
        pl.semaphore_signal(
            barrier, inc=1, device_id=((me + j) % count, now), device_id_type=pl.DeviceIdType.MESH
        )
    for j in range(1, steps):
        pl.semaphore_signal(
            barrier, inc=1, device_id=(me, (now + j) % steps), device_id_type=pl.DeviceIdType.MESH
        )

    def send(src, dst, send_sem, recv_sem, row, step):
        return pltpu.make_async_remote_copy(
            src_ref=src, dst_ref=dst, send_sem=send_sem, recv_sem=recv_sem,
            device_id=(row, step), device_id_type=pl.DeviceIdType.MESH,
        )

    width = jac_ref.shape[2]
    blocks = width // LANES
    tiles = [{}, {}]

    def gram(i):
        lo, hi = i * LANES, (i + 1) * LANES
        first, second = [
            lax.dot_general(
                jac_ref[s, :, lo:hi], jac_ref[s, :, lo:], (((0,), (0,)), ((), ())),
                preferred_element_type=jnp.float32,
            )
            for s in range(2)
        ]
        second = keep1 * first + second
        for j in range(i, blocks):
            left = (j - i) * LANES
            tiles[0][i, j] = first[:, left : left + LANES]
            tiles[1][i, j] = second[:, left : left + LANES]

    def pack(names, part_ref):
        every = count // len(names)
        for s in range(2):
            for q, (i, j, square) in enumerate(names):
                tile = tiles[s][i, j]
                if square:
                    tile = jnp.where(lane > sub, tiles[s][i, i], tiles[s][j, j])
                for k in range(every):
                    part_ref[q * every + k, s, :part, :] = tile[k * part : (k + 1) * part, :]

    def pack_vectors(part_ref):
        vecs = [
            jnp.dot(rhs_ref[s : s + 1, :], jac_ref[s], preferred_element_type=jnp.float32) for s in range(2)
        ]
        vecs[1] = keep1 * vecs[0] + vecs[1]
        for s in range(2):
            extra = [vecs[s][:, lo : lo + LANES] for lo in range(0, width, LANES)]
            extra.append(jnp.sum(jnp.where(lane == sub, tiles[s][0, 0], 0.0), axis=0, keepdims=True))
            extra.append(jnp.sum(jnp.where(lane == sub, tiles[s][2, 2], 0.0), axis=0, keepdims=True))
            extra.append(jnp.zeros((GROUP - len(extra), LANES), jnp.float32))
            part_ref[0, s, part:, :] = jnp.concatenate(extra, axis=0)
            for owner in range(1, count):
                part_ref[owner, s, part:, :] = jnp.zeros((GROUP, LANES), jnp.float32)

    order = list(range(1, half)) + [0]
    first, second, passed, last = [({}, {}) for _ in range(4)]

    def pair_start(c):
        part_ref, near, near_send, near_recv = (chunks[c][0], chunks[c][1], chunks[c][8], chunks[c][9])
        for j in order:
            owner = 2 * ((line + j) % half) + (1 - side)
            first[c][j] = send(
                part_ref.at[owner], near.at[j], near_send.at[j], near_recv.at[j], other_row, now
            )
            first[c][j].start()

    def pair_finish(c, places):
        part_ref, near, far, far_send, far_recv = chunks[c][:3] + chunks[c][10:12]
        for j in places:
            first[c][j].wait_recv()
            owner = 2 * ((line + j) % half) + side
            near[j] = near[j] + part_ref[owner]
            if j:
                second[c][j] = send(near.at[j], far.at[j], far_send.at[j], far_recv.at[j], owner, now)
                second[c][j].start()

    def pass_on(c):
        near, far, mine, past, past_send, past_recv = chunks[c][1:5] + chunks[c][12:14]
        total = near[0]
        for j in range(1, half):
            second[c][j].wait_recv()
            total = total + far[j]
        size = total.shape[1]
        mine[:, :size, :] = total
        mine[:, size:, :] = jnp.full((2, GROUP, LANES), keep0 * keep1, jnp.float32)
        for j in range(1, steps):
            passed[c][j] = send(
                mine.at[1], past.at[j], past_send.at[j], past_recv.at[j], me, (now + j) % steps
            )

            @pl.when(now + j < steps)
            def _(j=j):
                passed[c][j].start()

    def spread(c):
        mine, past, post, prior, whole, last_send, last_recv = chunks[c][3:8] + chunks[c][14:16]
        size = post.shape[1]
        prior[...] = jnp.zeros_like(prior)
        weight[...] = jnp.ones_like(weight)
        for j in range(1, steps):
            @pl.when(now >= j)
            def _(j=j):
                passed[c][j].wait_recv()
                prior[...] = prior[...] + weight[0:1, :] * past[j, :size, :]
                weight[...] = weight[...] * past[j, size:, :]

        post[0] = keep0 * prior[...] + mine[0, :size, :]
        post[1] = (keep0 * keep1) * prior[...] + mine[1, :size, :]
        for j in range(1, count):
            other = (me + j) % count
            last[c][j] = send(
                post.at[other % 2], whole.at[me], last_send.at[j], last_recv.at[j], other, now
            )

            @pl.when(inner(other))
            def _(j=j):
                last[c][j].start()

        whole[me] = post[side]

    gram(0)
    gram(1)
    pack(EARLY, chunks[0][0])
    gram(2)
    pack_vectors(chunks[0][0])
    pl.semaphore_wait(barrier, count + steps - 2)
    pair_start(0)
    gram(3)
    pack(LATE, chunks[1][0])
    pair_start(1)
    pair_finish(0, order)
    pair_finish(1, order[: half // 2])
    pass_on(0)
    pair_finish(1, order[half // 2 :])
    spread(0)
    pass_on(1)
    spread(1)
    front, back = chunks[0][7], chunks[1][7]
    tiles = LANES // GROUP

    def unpack(names, source):
        every = count // len(names)
        for q, (i, j, square) in enumerate(names):
            tile = jnp.concatenate([source[q * every + k, :part, :] for k in range(every)], axis=0)
            if square:
                diagonal = front[0, part + blocks + i // 2 : part + blocks + i // 2 + 1, :]
                over = jnp.where(lane > sub, tile, 0.0)
                under = jnp.where(lane < sub, tile, 0.0)
                work[i * LANES : (i + 1) * LANES, i * LANES : (i + 1) * LANES] = (
                    over + over.T + jnp.where(lane == sub, diagonal, 0.0)
                )
                work[j * LANES : (j + 1) * LANES, j * LANES : (j + 1) * LANES] = tile - over + under.T
            else:
                work[i * LANES : (i + 1) * LANES, j * LANES : (j + 1) * LANES] = tile

    row_share = rows_ref.shape[1]

    def rows_to(k, i):
        start = pl.multiple_of(takers[k] * row_share, GROUP)
        return send(
            work.at[pl.ds(start, row_share), pl.ds(i * LANES, width - i * LANES)],
            rows_ref.at[side, :, pl.ds(i * LANES, width - i * LANES)],
            rows_send.at[k], rows_recv.at[side], takers[k], now,
        )

    def state_to(k):
        return send(vec, state_ref.at[side], state_send.at[k], state_recv.at[side], takers[k], now)

    def give_rows(i):
        for k in range(3):
            @pl.when((takers[k] * row_share) // LANES == i)
            def _(k=k):
                rows_to(k, i).start()

    for i in range(1, blocks):
        @pl.when((me * row_share) // LANES == i)
        def _(i=i):
            rows_ref[:, :, : i * LANES] = jnp.zeros((2, row_share, i * LANES), jnp.float32)

    @pl.when(factors)
    def _():
        for j in range(1, count):
            last[0][j].wait_recv()
        unpack(EARLY, front)
        for j in range(blocks):
            vec[:, j * LANES : (j + 1) * LANES] = jnp.broadcast_to(
                front[0, part + j : part + j + 1, :], (GROUP, LANES)
            )

        def block_step(b, carry):
            base = pl.multiple_of(b * LANES, LANES)

            def place(t):
                return pl.ds(pl.multiple_of(base + t * GROUP, GROUP), GROUP)

            upper, lower = factor_tiles([[work[place(t), pl.ds(base, LANES)] for t in range(tiles)]])
            for t in range(tiles):
                work[place(t), pl.ds(base, LANES)] = upper[0][t]
                inv[place(t), :] = lower[0][t]

            for i in range(blocks):
                @pl.when(b == i)
                def _(i=i):
                    lo, hi = i * LANES, (i + 1) * LANES
                    low = inv[lo:hi, :]
                    y = dot(vec[:, lo:hi], low, 1, 1)
                    vec[:, lo:hi] = y
                    if i < blocks - 1:
                        panel = dot(low, work[lo:hi, hi:], 1, 0)
                        work[lo:hi, hi:] = panel
                        vec[:, hi:] = vec[:, hi:] - dot(y, panel, 1, 0)
                    give_rows(i)
                    if i < blocks - 1:
                        if i == 0:
                            for j in range(1, count):
                                last[1][j].wait_recv()
                            unpack(LATE, back)
                        for j in range(i + 1, blocks):
                            left = (j - i - 1) * LANES
                            jl, jh = j * LANES, (j + 1) * LANES
                            work[jl:jh, jl:] = work[jl:jh, jl:] - dot(
                                panel[:, left : left + LANES], panel[:, left:], 0, 0
                            )
                            work[jl:jh, lo:hi] = jnp.zeros((LANES, LANES), jnp.float32)

            return carry

        lax.fori_loop(0, blocks, block_step, 0)
        for b in reversed(range(blocks)):
            lo, hi = b * LANES, (b + 1) * LANES
            right = vec[:, lo:hi]
            if b < blocks - 1:
                right = right - dot(vec[:, hi:], work[lo:hi, hi:], 1, 1)
            vec[:, lo:hi] = dot(right, inv[lo:hi, :], 1, 0)
        for k in range(3):
            state_to(k).start()
        for i in range(blocks):
            @pl.when((me * row_share) // LANES == i)
            def _(i=i):
                start = pl.multiple_of(me * row_share, GROUP)
                rows_ref[side, :, i * LANES :] = work[pl.ds(start, row_share), i * LANES :]
        state_ref[side] = vec[...]
        for k in range(3):
            for i in range(blocks):
                @pl.when((takers[k] * row_share) // LANES == i)
                def _(k=k, i=i):
                    rows_to(k, i).wait_send()
            state_to(k).wait_send()

    for s in range(2):
        @pl.when(jnp.logical_or(jnp.logical_not(factors), side != s))
        def _(s=s):
            for i in range(blocks):
                @pl.when((me * row_share) // LANES == i)
                def _(i=i):
                    kept = rows_ref.at[s, :, pl.ds(i * LANES, width - i * LANES)]
                    send(kept, kept, rows_send.at[0], rows_recv.at[s], other_row, now).wait_recv()
            kept = state_ref.at[s]
            send(kept, kept, state_send.at[0], state_recv.at[s], other_row, now).wait_recv()

    for c in range(2):
        for j in order:
            first[c][j].wait_send()
            if j:
                second[c][j].wait_send()
        for j in range(1, steps):
            @pl.when(now + j < steps)
            def _(j=j):
                passed[c][j].wait_send()
        for j in range(1, count):
            @pl.when(inner((me + j) % count))
            def _(j=j):
                last[c][j].wait_send()


def smooth(forget, restart, jacobian, rhs, count, steps):
    width = jacobian.shape[2]
    part, early, _ = shard_rows(count)
    half = count // 2
    vmem = pl.BlockSpec(memory_space=pltpu.VMEM)
    smem = pl.BlockSpec(memory_space=pltpu.SMEM)
    dma = pltpu.SemaphoreType.DMA
    f32 = jnp.float32
    scratch = []
    for size in (early, part):
        scratch += [
            pltpu.VMEM((count, 2, size, LANES), f32),
            pltpu.VMEM((half, 2, size, LANES), f32),
            pltpu.VMEM((half, 2, size, LANES), f32),
            pltpu.VMEM((2, size + GROUP, LANES), f32),
            pltpu.VMEM((steps, size + GROUP, LANES), f32),
            pltpu.VMEM((2, size, LANES), f32),
            pltpu.VMEM((size, LANES), f32),
            pltpu.VMEM((count, size, LANES), f32),
            dma((half,)), dma((half,)), dma((half,)), dma((half,)),
            dma((steps,)), dma((steps,)), dma((count,)), dma((count,)),
        ]
    scratch += [
        pltpu.VMEM((GROUP, LANES), f32),
        pltpu.VMEM((width, width), f32),
        pltpu.VMEM((width, LANES), f32),
        pltpu.VMEM((GROUP, width), f32),
        dma((3,)), dma((2,)), dma((3,)), dma((2,)),
    ]
    return pl.pallas_call(
        functools.partial(smooth_kernel, count, steps),
        out_shape=(
            jax.ShapeDtypeStruct((2, width // count, width), f32),
            jax.ShapeDtypeStruct((2, GROUP, width), f32),
        ),
        in_specs=[smem, smem, vmem, vmem],
        out_specs=(vmem, vmem),
        scratch_shapes=scratch,
        compiler_params=pltpu.CompilerParams(
            collective_id=0, has_side_effects=True, vmem_limit_bytes=40 * 1024 * 1024
        ),
    )(forget, restart, jacobian, rhs)


def on_device(jacobian, rhs, forget, restart):
    count, steps = lax.axis_size("rows"), lax.axis_size("tm")
    row_share = jacobian.shape[2] // count
    factor, state = smooth(forget, restart, jacobian, rhs, count, steps)
    start = lax.axis_index("rows") * row_share
    return factor, lax.dynamic_slice_in_dim(state[:, 0, :], start, row_share, 1)


def solution(mesh):
    in_specs = (P("tm", "rows", None), P("tm", "rows"), P("tm"), P("tm"))
    out_specs = (P("tm", "rows", None), P("tm", "rows"))
    return jax.shard_map(
        on_device, mesh=mesh, in_specs=in_specs, out_specs=out_specs, check_vma=False
    )
```

```python
import functools

import jax
import jax.numpy as jnp
from jax import lax
from jax.experimental import pallas as pl
from jax.experimental.pallas import tpu as pltpu
from jax.sharding import PartitionSpec as P

HIGHEST = lax.Precision.HIGHEST
LANES = 128
GROUP = 8


def dot(a, b, over_a, over_b):
    return lax.dot_general(
        a, b, (((over_a,), (over_b,)), ((), ())),
        precision=HIGHEST, preferred_element_type=jnp.float32,
    )


def lane_spread(tile, lane):
    return jnp.broadcast_to(tile[:, lane : lane + 1], tile.shape)


def row_spread(tile, row):
    return jnp.broadcast_to(tile[row : row + 1, :], tile.shape)


def factor_tiles(many):
    lane = lax.broadcasted_iota(jnp.int32, (GROUP, LANES), 1)
    sub = lax.broadcasted_iota(jnp.int32, (GROUP, LANES), 0)
    many = [list(tiles) for tiles in many]
    count = len(many[0])
    here = range(len(many))
    over = [jnp.ones((GROUP, LANES), jnp.float32) for _ in here]
    pivots = [[None] * count for _ in here]
    for g in range(count):
        top = [many[s][g] for s in here]
        cols = [[lane_spread(top[s], g * GROUP + k) for k in range(GROUP)] for s in here]
        inverse = [[None] * GROUP for _ in here]
        rows = [[None] * GROUP for _ in here]
        heads = [[None] * GROUP for _ in here]
        for k in range(GROUP):
            at = g * GROUP + k
            for s in here:
                head = [None] * (k + 1) + [row_spread(c, k) for c in cols[s][k + 1 :]]
                pivot = row_spread(cols[s][k], k)
                inv = 1.0 / pivot
                times = jnp.where(sub > k, cols[s][k] * inv, 0.0)
                row = row_spread(top[s], k)
                row = jnp.where(lane == at, row + row, row)
                top[s] = top[s] - times * row
                for later in range(k + 1, GROUP):
                    cols[s][later] = cols[s][later] - times * head[later]
                inverse[s][k], rows[s][k], heads[s][k] = inv, row, head
                over[s] = jnp.where(lane == at, inv, over[s])
                pivots[s][g] = pivot if k == 0 else jnp.where(sub >= k, pivot, pivots[s][g])
        for s in here:
            many[s][g] = top[s]
        turned = []
        for s in here:
            scaled = top[s] * inverse[s][0]
            for k in range(1, GROUP):
                scaled = jnp.where(sub >= k, top[s] * inverse[s][k], scaled)
            turned.append(scaled.T)
        for v in range(g + 2, count):
            for s in here:
                tile = many[s][v]
                for k in range(GROUP):
                    times = turned[s][v * GROUP : (v + 1) * GROUP, k : k + 1]
                    tile = tile - jnp.broadcast_to(times, tile.shape) * rows[s][k]
                many[s][v] = tile
        for v in range(g + 1, min(g + 2, count)):
            for s in here:
                tile = many[s][v]
                mine = [lane_spread(tile, g * GROUP + k) for k in range(GROUP)]
                for k in range(GROUP):
                    times = mine[k] * inverse[s][k]
                    tile = tile - times * rows[s][k]
                    for later in range(k + 1, GROUP):
                        mine[later] = mine[later] - times * heads[s][k][later]
                many[s][v] = tile
    upper, lower = [], []
    for s in here:
        ups, lows = [], []
        for g in range(count):
            scale = lax.rsqrt(pivots[s][g])
            tile = many[s][g] * scale
            at = sub + g * GROUP
            ups.append(jnp.where(lane >= at, tile, 0.0))
            lows.append(jnp.where(lane <= at, tile * over[s], 0.0))
        upper.append(ups)
        lower.append(lows)
    return upper, lower


EARLY = ((0, 1, True), (0, 1, False), (0, 2, False), (0, 3, False))
LATE = ((1, 2, False), (1, 3, False), (2, 3, False), (2, 3, True))


def shard_rows(count):
    part = len(EARLY) * LANES // count
    return part, part + GROUP, 2 * part + GROUP


def smooth_kernel(count, steps, forget_ref, restart_ref, jac_ref, rhs_ref, rows_ref, state_ref, *scratch):
    chunks = (scratch[:16], scratch[16:32])
    weight, work, inv, vec, rows_send, rows_recv, state_send, state_recv = scratch[32:]
    me, now = lax.axis_index("rows"), lax.axis_index("tm")
    half = count // 2
    part, early, share = shard_rows(count)
    line, side = me // 2, me % 2
    other_row = me + 1 - 2 * side

    def inner(row):
        return jnp.logical_or((row // 2) % 4 == 1, (row // 2) % 4 == 2)

    factors = inner(me)
    guest = 2 * jnp.where(line % 4 == 1, line - 1, jnp.minimum(line + 1, half - 1))
    takers = (other_row, guest, guest + 1)
    keep0, keep1 = [forget_ref[k] * (1.0 - 0.2 * restart_ref[k].astype(jnp.float32)) for k in range(2)]
    lane = lax.broadcasted_iota(jnp.int32, (LANES, LANES), 1)
    sub = lax.broadcasted_iota(jnp.int32, (LANES, LANES), 0)

    barrier = pltpu.get_barrier_semaphore()
    for j in range(1, count):
        pl.semaphore_signal(
            barrier, inc=1, device_id=((me + j) % count, now), device_id_type=pl.DeviceIdType.MESH
        )
    for j in range(1, steps):
        pl.semaphore_signal(
            barrier, inc=1, device_id=(me, (now + j) % steps), device_id_type=pl.DeviceIdType.MESH
        )

    def send(src, dst, send_sem, recv_sem, row, step):
        return pltpu.make_async_remote_copy(
            src_ref=src, dst_ref=dst, send_sem=send_sem, recv_sem=recv_sem,
            device_id=(row, step), device_id_type=pl.DeviceIdType.MESH,
        )

    width = jac_ref.shape[2]
    blocks = width // LANES
    tiles = [{}, {}]

    def gram(i):
        lo, hi = i * LANES, (i + 1) * LANES
        first, second = [
            lax.dot_general(
                jac_ref[s, :, lo:hi], jac_ref[s, :, lo:], (((0,), (0,)), ((), ())),
                preferred_element_type=jnp.float32,
            )
            for s in range(2)
        ]
        second = keep1 * first + second
        for j in range(i, blocks):
            left = (j - i) * LANES
            tiles[0][i, j] = first[:, left : left + LANES]
            tiles[1][i, j] = second[:, left : left + LANES]

    def pack(names, part_ref):
        every = count // len(names)
        for s in range(2):
            for q, (i, j, square) in enumerate(names):
                tile = tiles[s][i, j]
                if square:
                    tile = jnp.where(lane > sub, tiles[s][i, i], tiles[s][j, j])
                for k in range(every):
                    part_ref[q * every + k, s, :part, :] = tile[k * part : (k + 1) * part, :]

    def pack_vectors(part_ref):
        vecs = [
            jnp.dot(rhs_ref[s : s + 1, :], jac_ref[s], preferred_element_type=jnp.float32) for s in range(2)
        ]
        vecs[1] = keep1 * vecs[0] + vecs[1]
        for s in range(2):
            extra = [vecs[s][:, lo : lo + LANES] for lo in range(0, width, LANES)]
            extra.append(jnp.sum(jnp.where(lane == sub, tiles[s][0, 0], 0.0), axis=0, keepdims=True))
            extra.append(jnp.sum(jnp.where(lane == sub, tiles[s][2, 2], 0.0), axis=0, keepdims=True))
            extra.append(jnp.zeros((GROUP - len(extra), LANES), jnp.float32))
            part_ref[0, s, part:, :] = jnp.concatenate(extra, axis=0)
            for owner in range(1, count):
                part_ref[owner, s, part:, :] = jnp.zeros((GROUP, LANES), jnp.float32)

    order = list(range(1, half)) + [0]
    first, second, passed, last = [({}, {}) for _ in range(4)]

    def pair_start(c):
        part_ref, near, near_send, near_recv = (chunks[c][0], chunks[c][1], chunks[c][8], chunks[c][9])
        for j in order:
            owner = 2 * ((line + j) % half) + (1 - side)
            first[c][j] = send(
                part_ref.at[owner], near.at[j], near_send.at[j], near_recv.at[j], other_row, now
            )
            first[c][j].start()

    def pair_finish(c, places):
        part_ref, near, far, far_send, far_recv = chunks[c][:3] + chunks[c][10:12]
        for j in places:
            first[c][j].wait_recv()
            owner = 2 * ((line + j) % half) + side
            near[j] = near[j] + part_ref[owner]
            if j:
                second[c][j] = send(near.at[j], far.at[j], far_send.at[j], far_recv.at[j], owner, now)
                second[c][j].start()

    def pass_on(c):
        near, far, mine, past, past_send, past_recv = chunks[c][1:5] + chunks[c][12:14]
        total = near[0]
        for j in range(1, half):
            second[c][j].wait_recv()
            total = total + far[j]
        size = total.shape[1]
        mine[:, :size, :] = total
        mine[:, size:, :] = jnp.full((2, GROUP, LANES), keep0 * keep1, jnp.float32)
        for j in range(1, steps):
            passed[c][j] = send(
                mine.at[1], past.at[j], past_send.at[j], past_recv.at[j], me, (now + j) % steps
            )

            @pl.when(now + j < steps)
            def _(j=j):
                passed[c][j].start()

    def spread(c):
        mine, past, post, prior, whole, last_send, last_recv = chunks[c][3:8] + chunks[c][14:16]
        size = post.shape[1]
        prior[...] = jnp.zeros_like(prior)
        weight[...] = jnp.ones_like(weight)
        for j in range(1, steps):
            @pl.when(now >= j)
            def _(j=j):
                passed[c][j].wait_recv()
                prior[...] = prior[...] + weight[0:1, :] * past[j, :size, :]
                weight[...] = weight[...] * past[j, size:, :]

        post[0] = keep0 * prior[...] + mine[0, :size, :]
        post[1] = (keep0 * keep1) * prior[...] + mine[1, :size, :]
        for j in range(1, count):
            other = (me + j) % count
            last[c][j] = send(
                post.at[other % 2], whole.at[me], last_send.at[j], last_recv.at[j], other, now
            )

            @pl.when(inner(other))
            def _(j=j):
                last[c][j].start()

        whole[me] = post[side]

    gram(0)
    gram(1)
    pack(EARLY, chunks[0][0])
    gram(2)
    pack_vectors(chunks[0][0])
    pl.semaphore_wait(barrier, count + steps - 2)
    pair_start(0)
    gram(3)
    pack(LATE, chunks[1][0])
    pair_start(1)
    pair_finish(0, order)
    pair_finish(1, order[: half // 2])
    pass_on(0)
    pair_finish(1, order[half // 2 :])
    spread(0)
    pass_on(1)
    spread(1)
    front, back = chunks[0][7], chunks[1][7]
    tiles = LANES // GROUP

    def unpack(names, source):
        every = count // len(names)
        for q, (i, j, square) in enumerate(names):
            tile = jnp.concatenate([source[q * every + k, :part, :] for k in range(every)], axis=0)
            if square:
                diagonal = front[0, part + blocks + i // 2 : part + blocks + i // 2 + 1, :]
                over = jnp.where(lane > sub, tile, 0.0)
                under = jnp.where(lane < sub, tile, 0.0)
                work[i * LANES : (i + 1) * LANES, i * LANES : (i + 1) * LANES] = (
                    over + over.T + jnp.where(lane == sub, diagonal, 0.0)
                )
                work[j * LANES : (j + 1) * LANES, j * LANES : (j + 1) * LANES] = tile - over + under.T
            else:
                work[i * LANES : (i + 1) * LANES, j * LANES : (j + 1) * LANES] = tile

    row_share = rows_ref.shape[1]

    def rows_to(k, i):
        start = pl.multiple_of(takers[k] * row_share, GROUP)
        return send(
            work.at[pl.ds(start, row_share), pl.ds(i * LANES, width - i * LANES)],
            rows_ref.at[side, :, pl.ds(i * LANES, width - i * LANES)],
            rows_send.at[k], rows_recv.at[side], takers[k], now,
        )

    def state_to(k):
        return send(vec, state_ref.at[side], state_send.at[k], state_recv.at[side], takers[k], now)

    def give_rows(i):
        for k in range(3):
            @pl.when((takers[k] * row_share) // LANES == i)
            def _(k=k):
                rows_to(k, i).start()

    for i in range(1, blocks):
        @pl.when((me * row_share) // LANES == i)
        def _(i=i):
            rows_ref[:, :, : i * LANES] = jnp.zeros((2, row_share, i * LANES), jnp.float32)

    @pl.when(factors)
    def _():
        for j in range(1, count):
            last[0][j].wait_recv()
        unpack(EARLY, front)
        for j in range(blocks):
            vec[:, j * LANES : (j + 1) * LANES] = jnp.broadcast_to(
                front[0, part + j : part + j + 1, :], (GROUP, LANES)
            )

        def block_step(b, carry):
            base = pl.multiple_of(b * LANES, LANES)

            def place(t):
                return pl.ds(pl.multiple_of(base + t * GROUP, GROUP), GROUP)

            upper, lower = factor_tiles([[work[place(t), pl.ds(base, LANES)] for t in range(tiles)]])
            for t in range(tiles):
                work[place(t), pl.ds(base, LANES)] = upper[0][t]
                inv[place(t), :] = lower[0][t]

            for i in range(blocks):
                @pl.when(b == i)
                def _(i=i):
                    lo, hi = i * LANES, (i + 1) * LANES
                    low = inv[lo:hi, :]
                    y = dot(vec[:, lo:hi], low, 1, 1)
                    vec[:, lo:hi] = y
                    if i < blocks - 1:
                        panel = dot(low, work[lo:hi, hi:], 1, 0)
                        work[lo:hi, hi:] = panel
                        vec[:, hi:] = vec[:, hi:] - dot(y, panel, 1, 0)
                    give_rows(i)
                    if i < blocks - 1:
                        if i == 0:
                            for j in range(1, count):
                                last[1][j].wait_recv()
                            unpack(LATE, back)
                        for j in range(i + 1, blocks):
                            left = (j - i - 1) * LANES
                            jl, jh = j * LANES, (j + 1) * LANES
                            work[jl:jh, jl:] = work[jl:jh, jl:] - dot(
                                panel[:, left : left + LANES], panel[:, left:], 0, 0
                            )
                            work[jl:jh, lo:hi] = jnp.zeros((LANES, LANES), jnp.float32)

            return carry

        lax.fori_loop(0, blocks, block_step, 0)
        for b in reversed(range(blocks)):
            lo, hi = b * LANES, (b + 1) * LANES
            right = vec[:, lo:hi]
            if b < blocks - 1:
                right = right - dot(vec[:, hi:], work[lo:hi, hi:], 1, 1)
            vec[:, lo:hi] = dot(right, inv[lo:hi, :], 1, 0)
        for k in range(3):
            state_to(k).start()
        for i in range(blocks):
            @pl.when((me * row_share) // LANES == i)
            def _(i=i):
                start = pl.multiple_of(me * row_share, GROUP)
                rows_ref[side, :, i * LANES :] = work[pl.ds(start, row_share), i * LANES :]
        state_ref[side] = vec[...]
        for k in range(3):
            for i in range(blocks):
                @pl.when((takers[k] * row_share) // LANES == i)
                def _(k=k, i=i):
                    rows_to(k, i).wait_send()
            state_to(k).wait_send()

    for s in range(2):
        @pl.when(jnp.logical_or(jnp.logical_not(factors), side != s))
        def _(s=s):
            for i in range(blocks):
                @pl.when((me * row_share) // LANES == i)
                def _(i=i):
                    kept = rows_ref.at[s, :, pl.ds(i * LANES, width - i * LANES)]
                    send(kept, kept, rows_send.at[0], rows_recv.at[s], other_row, now).wait_recv()
            kept = state_ref.at[s]
            send(kept, kept, state_send.at[0], state_recv.at[s], other_row, now).wait_recv()

    for c in range(2):
        for j in order:
            first[c][j].wait_send()
            if j:
                second[c][j].wait_send()
        for j in range(1, steps):
            @pl.when(now + j < steps)
            def _(j=j):
                passed[c][j].wait_send()
        for j in range(1, count):
            @pl.when(inner((me + j) % count))
            def _(j=j):
                last[c][j].wait_send()


def smooth(forget, restart, jacobian, rhs, count, steps):
    width = jacobian.shape[2]
    part, early, _ = shard_rows(count)
    half = count // 2
    vmem = pl.BlockSpec(memory_space=pltpu.VMEM)
    smem = pl.BlockSpec(memory_space=pltpu.SMEM)
    dma = pltpu.SemaphoreType.DMA
    f32 = jnp.float32
    scratch = []
    for size in (early, part):
        scratch += [
            pltpu.VMEM((count, 2, size, LANES), f32),
            pltpu.VMEM((half, 2, size, LANES), f32),
            pltpu.VMEM((half, 2, size, LANES), f32),
            pltpu.VMEM((2, size + GROUP, LANES), f32),
            pltpu.VMEM((steps, size + GROUP, LANES), f32),
            pltpu.VMEM((2, size, LANES), f32),
            pltpu.VMEM((size, LANES), f32),
            pltpu.VMEM((count, size, LANES), f32),
            dma((half,)), dma((half,)), dma((half,)), dma((half,)),
            dma((steps,)), dma((steps,)), dma((count,)), dma((count,)),
        ]
    scratch += [
        pltpu.VMEM((GROUP, LANES), f32),
        pltpu.VMEM((width, width), f32),
        pltpu.VMEM((width, LANES), f32),
        pltpu.VMEM((GROUP, width), f32),
        dma((3,)), dma((2,)), dma((3,)), dma((2,)),
    ]
    return pl.pallas_call(
        functools.partial(smooth_kernel, count, steps),
        out_shape=(
            jax.ShapeDtypeStruct((2, width // count, width), f32),
            jax.ShapeDtypeStruct((2, GROUP, width), f32),
        ),
        in_specs=[smem, smem, vmem, vmem],
        out_specs=(vmem, vmem),
        scratch_shapes=scratch,
        compiler_params=pltpu.CompilerParams(
            collective_id=0, has_side_effects=True, vmem_limit_bytes=40 * 1024 * 1024
        ),
    )(forget, restart, jacobian, rhs)


def on_device(jacobian, rhs, forget, restart):
    count, steps = lax.axis_size("rows"), lax.axis_size("tm")
    row_share = jacobian.shape[2] // count
    factor, state = smooth(forget, restart, jacobian, rhs, count, steps)
    start = lax.axis_index("rows") * row_share
    return factor, lax.dynamic_slice_in_dim(state[:, 0, :], start, row_share, 1)


def solution(mesh):
    in_specs = (P("tm", "rows", None), P("tm", "rows"), P("tm"), P("tm"))
    out_specs = (P("tm", "rows", None), P("tm", "rows"))
    return jax.shard_map(
        on_device, mesh=mesh, in_specs=in_specs, out_specs=out_specs, check_vma=False
    )
```
